256 devices in a mesh: gx: 32 (over x_lo, z, core), gz: 8 (over y, x_hi).
Axes of the slice: x: 4 (x_hi: 2, x_lo: 2; x = x_hi * 2 + x_lo), y: 4, z: 8, core: 2. Of those that a mesh axis runs over, the one named last changes fastest.
Arguments:
- velocity: float32 [3, 256, 256, 128], P(None, 'gx', 'gz'), may hold values from -12 to 12
- eddy_viscosity: float32 [4, 256, 256], P(None, 'gx', 'gz'), may hold values from 0.02 to 0.5
- target_spectrum: float32 [256], replicated, may hold values from 0.5 to 4
- mean_profile: float32 [128], replicated, may hold values from 0 to 2
- past_rewards: float32 [12, 256, 256], P(None, 'gx', 'gz'), may hold values from -6 to 6
- bootstrap_values: float32 [256, 256], P('gx', 'gz'), may hold values from -12 to 12
Outputs:
- final_velocity: float32 [3, 256, 256, 128], P(None, 'gx', 'gz')
- discounted_returns: float32 [16, 256, 256], P(None, 'gx', 'gz')
The draws below stay inside these ranges and needn't reach their ends.
All inputs are finite; a program needn't handle non-finite values.
Results may differ from the reference program's by a relative error of at most 0.0001.
Values sent between devices are 32-bit elements; how exact they have to be, the bound alone decides.
A program may use at most 64 MiB of HBM per device.

```python
import math
import jax
import jax.numpy as jnp
from jax import lax

NY = 128
STEPS = 4
HORIZON = 16
KX = 16
KZ = 16
PAST = 12
NX = 256
NZ = 256


def wave_tables(waves, total):
    turns = jnp.arange(waves).astype(jnp.int32)[:, None] * jnp.arange(total).astype(jnp.int32)[None, :] % total
    angle = turns.astype(jnp.float32) * (2.0 * math.pi / total)
    return (jnp.cos(angle), jnp.sin(angle))


def draw_velocity(key, part):
    key = jax.random.fold_in(key, 11)
    key_factor = jax.random.fold_in(key, 1)
    key_first = jax.random.fold_in(key, 2)
    key_second = jax.random.fold_in(key, 3)
    key_noise = jax.random.fold_in(key, 4)
    high = lax.Precision.HIGHEST
    along_x = 0.6 + 0.8 * jnp.arange(NX).astype(jnp.float32) / NX
    along_z = 0.6 + 0.8 * jnp.arange(NZ).astype(jnp.float32) / NZ
    envelope = along_x[:, None, None] * along_z[None, :, None]
    index_x = jnp.arange(NX).astype(jnp.int32)
    index_z = jnp.arange(NZ).astype(jnp.int32)
    index_y = jnp.arange(NY).astype(jnp.int32)
    parity_sum = (index_x[:, None, None] + index_z[None, :, None] + index_y[None, None, :]) % 2
    checker = 1.0 - 2.0 * parity_sum.astype(jnp.float32)
    wave_x = jnp.arange(KX).astype(jnp.float32)
    wave_z = jnp.arange(KZ).astype(jnp.float32)
    radius = 1.0 + (wave_x[:, None] ** 2 + wave_z[None, :] ** 2) / 16.0
    spread = jnp.exp(jax.random.uniform(key_factor, (KX, KZ), jnp.float32, math.log(0.35), math.log(2.8)))
    energy = 6.0 * radius ** (-5.0 / 6.0) * spread
    amplitude = jnp.sqrt(energy / (1.5 * NX * NZ))
    first = jnp.clip(jax.random.normal(key_first, (KX, KZ, 3, NY), jnp.float32), -4.0, 4.0)
    second = jnp.clip(jax.random.normal(key_second, (KX, KZ, 3, NY), jnp.float32), -4.0, 4.0)
    magnitude = 2.5 + 0.5 * jnp.clip(jax.random.normal(key_noise, (3, NX, NZ, NY), jnp.float32), -3.0, 3.0)
    component_scale = jnp.array([0.25, 1.0, 1.0], jnp.float32)[:, None, None, None]
    noise = component_scale * magnitude * checker[None]
    cos_part = first * amplitude[:, :, None, None]
    sin_part = second * amplitude[:, :, None, None]
    cos_x, sin_x = wave_tables(KX, NX)
    cos_z, sin_z = wave_tables(KZ, NZ)
    upper = jnp.einsum('klcy,lz->kczy', cos_part, cos_z, precision=high) + jnp.einsum('klcy,lz->kczy', sin_part, sin_z, precision=high)
    lower = jnp.einsum('klcy,lz->kczy', sin_part, cos_z, precision=high) - jnp.einsum('klcy,lz->kczy', cos_part, sin_z, precision=high)
    waves = jnp.einsum('kx,kczy->cxzy', cos_x, upper, precision=high) + jnp.einsum('kx,kczy->cxzy', sin_x, lower, precision=high)
    field = waves + noise * envelope[None]
    return jnp.clip(field, -12.0, 12.0)


def draw_eddy_viscosity(key, part):
    key = jax.random.fold_in(key, 23)
    key_parity = jax.random.fold_in(key, 1)
    key_strong = jax.random.fold_in(key, 2)
    key_weak = jax.random.fold_in(key, 3)
    key_factor = jax.random.fold_in(key, 4)
    parity = jax.random.randint(key_parity, (), 0, 2).astype(jnp.int32)
    step_index = jnp.arange(STEPS).astype(jnp.int32)
    strong = (step_index + parity) % 2 == 0
    high_level = jnp.exp(jax.random.uniform(key_strong, (STEPS,), jnp.float32, math.log(0.38), math.log(0.45)))
    low_level = jnp.exp(jax.random.uniform(key_weak, (STEPS,), jnp.float32, math.log(0.037), math.log(0.045)))
    levels = jnp.where(strong, high_level, low_level)
    factor = jnp.exp(jax.random.uniform(key_factor, (STEPS, NX, NZ), jnp.float32, math.log(0.55), math.log(1.1)))
    return jnp.clip(levels[:, None, None] * factor, 0.02, 0.5)


def block_scale(key, dims, cuts, smallest, top_value):
    def one(axis_at, parts):
        draws = jax.random.uniform(jax.random.fold_in(jax.random.fold_in(key, 6), axis_at), (parts,), jnp.float32, smallest / len(cuts), top_value / len(cuts))
        return jnp.repeat(jnp.exp(draws), dims[axis_at] // parts).reshape((-1,) + (1,) * (len(dims) - axis_at - 1))

    gain = one(*cuts[0])
    for cut in cuts[1:]:
        gain = gain * one(*cut)
    return gain


def gaussian(key, dims, deviation, bound, cuts=(), kind=jnp.bfloat16):
    drawn = deviation * jax.random.normal(key, dims, jnp.float32)
    if cuts:
        drawn = drawn * block_scale(key, dims, cuts, -0.22, 0.18)
    return jnp.clip(drawn, -bound, bound).astype(kind)


def setup_inputs(seed: int = 0) -> dict:
    key_list = jax.random.split(jax.random.key(seed), 7)
    velocity = draw_velocity(jax.random.fold_in(key_list[6], 71), 0)
    eddy_viscosity = draw_eddy_viscosity(jax.random.fold_in(key_list[6], 71), 0)
    target_spectrum = jnp.clip(jnp.exp(jax.random.uniform(key_list[2], (KX * KZ,), jnp.float32, math.log(0.5), math.log(4.0))), 0.5, 4.0)
    mean_profile = jnp.clip(jax.random.uniform(key_list[3], (NY,), jnp.float32, 0.0, 2.0), 0.0, 2.0)
    past_rewards = gaussian(key_list[4], (PAST, NX, NZ), 1.0, 6.0, ((1, 32), (2, 8)), jnp.float32)
    bootstrap_values = gaussian(key_list[5], (NX, NZ), 3.0, 12.0, ((0, 32), (1, 8)), jnp.float32)
    return {"velocity": velocity, "eddy_viscosity": eddy_viscosity, "target_spectrum": target_spectrum, "mean_profile": mean_profile, "past_rewards": past_rewards, "bootstrap_values": bootstrap_values}


step_length = 0.05
base_viscosity = 0.02
drive_force = 0.5
discount = 0.97

def wall_shape(count):
    rows = jnp.arange(count).astype(jnp.float32) + 0.5
    return jnp.minimum(rows, count - rows) / (count / 2.0)

def phase_tables(waves, positions, total, factor):
    turns = jnp.arange(waves).astype(jnp.int32)[:, None] * positions[None, :] % total
    angle = turns.astype(jnp.float32) * (2.0 * math.pi / total)
    return (jnp.cos(angle) * factor, jnp.sin(angle) * factor)

def combine(center, x_plus, x_minus, z_plus, z_minus, viscous):
    padded = jnp.pad(center, ((0, 0), (0, 0), (0, 0), (1, 1)))
    y_plus = padded[:, :, :, 2:]
    y_minus = padded[:, :, :, :-2]
    grad_x = (x_plus - x_minus) * 0.5
    grad_z = (z_plus - z_minus) * 0.5
    grad_y = (y_plus - y_minus) * 0.5
    laplace = x_plus + x_minus + z_plus + z_minus + y_plus + y_minus - 6.0 * center
    carried = center[0][None] * grad_x + center[2][None] * grad_y + center[1][None] * grad_z
    forcing = jnp.array([drive_force, 0.0, 0.0], jnp.float32)[:, None, None, None]
    return -carried + viscous[None] * laplace + forcing

def advance(field, viscous, tendency):
    first = tendency(field, viscous)
    second = tendency(field + 0.5 * step_length * first, viscous)
    third = tendency(field + 0.5 * step_length * second, viscous)
    fourth = tendency(field + step_length * third, viscous)
    return field + step_length / 6.0 * (first + 2.0 * second + 2.0 * third + fourth)

def mode_sums(field, cos_x, sin_x, cos_z, sin_z):
    high = lax.Precision.HIGHEST
    part_c = jnp.einsum('kx,cxzy->kczy', cos_x, field, precision=high)
    part_s = jnp.einsum('kx,cxzy->kczy', sin_x, field, precision=high)
    real_part = jnp.einsum('kczy,lz->klcy', part_c, cos_z, precision=high) - jnp.einsum('kczy,lz->klcy', part_s, sin_z, precision=high)
    imag_part = -(jnp.einsum('kczy,lz->klcy', part_s, cos_z, precision=high) + jnp.einsum('kczy,lz->klcy', part_c, sin_z, precision=high))
    stacked = jnp.stack([real_part, imag_part], axis=2)
    return stacked.reshape(cos_x.shape[0] * cos_z.shape[0], 6, field.shape[3])

def spectral_terms(coefs, target):
    energy = lax.optimization_barrier(jnp.sum(coefs * coefs, axis=(-2, -1))) / coefs.shape[-1]
    ratio = (energy - target) / (energy + target)
    return ratio * ratio

def periodic_tendency(field, viscous):
    return combine(field, jnp.roll(field, -1, 1), jnp.roll(field, 1, 1), jnp.roll(field, -1, 2), jnp.roll(field, 1, 2), viscous)

def reference(velocity, eddy_viscosity, target_spectrum, mean_profile, past_rewards, bootstrap_values):
    factor = 1.0 / math.sqrt(NX * NZ)
    cos_x, sin_x = phase_tables(KX, jnp.arange(NX).astype(jnp.int32), NX, factor)
    cos_z, sin_z = phase_tables(KZ, jnp.arange(NZ).astype(jnp.int32), NZ, 1.0)
    wall = wall_shape(NY)
    field = velocity
    new_rewards = []
    for step in range(STEPS):
        viscous = base_viscosity + eddy_viscosity[step][:, :, None] * wall[None, None, :]
        field = advance(field, viscous, periodic_tendency)
        offset = field[0] - mean_profile[None, None, :]
        local = -lax.optimization_barrier(jnp.mean(offset * offset, axis=2))
        coefs = mode_sums(field, cos_x, sin_x, cos_z, sin_z)
        spectrum = -jnp.sum(spectral_terms(coefs, target_spectrum)) / KX
        new_rewards.append(local + spectrum)
    rewards = jnp.concatenate([past_rewards, jnp.stack(new_rewards)], axis=0)
    running = bootstrap_values
    outputs = []
    for index in range(HORIZON - 1, -1, -1):
        running = rewards[index] + discount * running
        outputs.append(running)
    return (field, jnp.stack(outputs[::-1]))
```

```python
import functools
import math

import numpy as np

import jax
import jax.numpy as jnp
from jax import lax
from jax.experimental import pallas as pl
from jax.experimental.pallas import tpu as pltpu
from jax.sharding import PartitionSpec as P

KX = 16
KZ = 16
STEP = 0.05
BASE_VISCOSITY = 0.02
DRIVE = 0.5
DISCOUNT = 0.97
HALO = 4
MESH = pl.DeviceIdType.MESH
HIGH = lax.Precision.HIGHEST


def z_table(peers, cells_x, cells_z, total_x, total_z):
    own = KZ // peers
    factor = 1.0 / math.sqrt(total_x * total_z)
    spots = np.arange(peers)[:, None] * cells_z + np.arange(cells_z)[None, :]
    turns = (np.arange(KZ)[None, :, None] * spots[:, None, :]) % total_z
    angle = turns * (2.0 * math.pi / total_z)
    waves = np.stack([np.cos(angle), -np.sin(angle)], axis=2) * factor
    eye = np.eye(cells_x)
    table = np.einsum("gkrz,ab->gkraBz".replace("B", "b"), waves, eye)
    rows = peers * own * 2 * cells_x
    return table.reshape(peers, rows, cells_x * cells_z).astype(np.float32)


def x_table(devices, peers, cells_x, total_x):
    own = KZ // peers
    spots = np.arange(devices)[:, None] * cells_x + np.arange(cells_x)[None, :]
    turns = (np.arange(KX)[None, :, None] * spots[:, None, :]) % total_x
    angle = turns * (2.0 * math.pi / total_x)
    c, s = np.cos(angle), np.sin(angle)
    spin = np.stack([np.stack([c, s], 2), np.stack([-s, c], 2)], 1)
    eye = np.eye(own)
    table = np.einsum("gqkrx,ab->gqkabrx", spin, eye)
    table = table.reshape(devices, 2 * KX * own, 1, own * 2 * cells_x)
    table = np.broadcast_to(table, (devices, 2 * KX * own, peers, own * 2 * cells_x))
    return table.reshape(devices, 2 * KX * own, peers * own * 2 * cells_x).astype(np.float32)


def kernel(
    ngx,
    ngz,
    vel,
    eddy,
    target,
    mean,
    past,
    boot,
    t1_hbm,
    t2_hbm,
    out_vel,
    out_ret,
    field,
    w2,
    w3,
    w4,
    nu,
    pack,
    zc,
    t1,
    t2,
    q_buf,
    r_buf,
    p_buf,
    s_buf,
    loc,
    term,
    a_buf,
    b_tile,
    b_buf,
    local_sem,
    halo_send,
    halo_recv,
    gz_send,
    gz_recv,
    gx_send,
    gx_recv,
    ar_send,
    ar_recv,
):
    gx = lax.axis_index("gx")
    gz = lax.axis_index("gz")
    steps = eddy.shape[0]
    nx = vel.shape[1]
    nz = vel.shape[2]
    ny = vel.shape[3]
    span = nz + 2 * HALO
    rows = (nx + 2 * HALO + 1) * span
    past_steps = past.shape[0]

    def xpeer(d):
        return lax.rem(gx + d + ngx, ngx)

    def zpeer(d):
        return lax.rem(gz + d + ngz, ngz)

    load_vel = pltpu.make_async_copy(
        vel, field.at[0, 0:3, pl.ds(HALO + 1, nx), 0:nz, :], local_sem.at[0]
    )
    load_t1 = pltpu.make_async_copy(t1_hbm.at[gz], t1, local_sem.at[1])
    load_t2 = pltpu.make_async_copy(t2_hbm.at[gx], t2, local_sem.at[2])
    load_vel.start()
    load_t1.start()
    load_t2.start()

    barrier = pltpu.get_barrier_semaphore()

    def greet_x(d, carry):
        pl.semaphore_signal(barrier, inc=1, device_id=(xpeer(d), gz), device_id_type=MESH)
        return carry

    def greet_z(d, carry):
        pl.semaphore_signal(barrier, inc=1, device_id=(gx, zpeer(d)), device_id_type=MESH)
        return carry

    lax.fori_loop(1, ngx, greet_x, 0)
    lax.fori_loop(1, ngz, greet_z, 0)
    for dx in (-1, 1):
        for dz in (-1, 1):
            pl.semaphore_signal(
                barrier, inc=1, device_id=(xpeer(dx), zpeer(dz)), device_id_type=MESH
            )

    eye = (
        lax.broadcasted_iota(jnp.int32, (steps, ny), 0)
        == lax.broadcasted_iota(jnp.int32, (steps, ny), 1)
    ).astype(jnp.float32)
    for x in range(nx):
        field[0, 3, HALO + 1 + x, 0:nz, :] = lax.dot_general(
            eddy[:, x, :],
            eye,
            (((0,), (0,)), ((), ())),
            precision=HIGH,
            preferred_element_type=jnp.float32,
        )

    def halo_copies(s, comps):
        copies = []
        first = HALO + 1
        for index, (dx, src, dst) in enumerate(
            ((1, first + nx - HALO, 1), (-1, first, first + nx))
        ):
            copies.append(
                pltpu.make_async_remote_copy(
                    src_ref=field.at[s, 0:comps, pl.ds(src, HALO), 0:nz, :],
                    dst_ref=field.at[s, 0:comps, pl.ds(dst, HALO), 0:nz, :],
                    send_sem=halo_send.at[s, index],
                    recv_sem=halo_recv.at[s, index],
                    device_id=(xpeer(dx), gz),
                    device_id_type=MESH,
                )
            )
        for side, dz in ((0, 1), (1, -1)):
            for index, (dx, src, dst, count) in enumerate(
                ((0, 0, HALO, nx), (1, nx - HALO, 0, HALO), (-1, 0, HALO + nx, HALO))
            ):
                copies.append(
                    pltpu.make_async_remote_copy(
                        src_ref=pack.at[s, side, 0:comps, pl.ds(src, count), :, :],
                        dst_ref=zc.at[s, side, 0:comps, pl.ds(dst, count), :, :],
                        send_sem=halo_send.at[s, 2 + 3 * side + index],
                        recv_sem=halo_recv.at[s, 2 + 3 * side + index],
                        device_id=(xpeer(dx), zpeer(dz)),
                        device_id_type=MESH,
                    )
                )
        return copies

    def start_halo(s, comps):
        first = HALO + 1
        for c in range(comps):
            pack[s, 0, c] = field[s, c, pl.ds(first, nx), nz - HALO : nz, :]
            pack[s, 1, c] = field[s, c, pl.ds(first, nx), 0:HALO, :]
        for copy in halo_copies(s, comps):
            copy.start()

    def wait_halo(s, comps):
        copies = halo_copies(s, comps)
        for copy in copies:
            copy.wait_recv()
        total = nx + 2 * HALO
        for c in range(comps):
            field[s, c, 0:total, nz + HALO : span, :] = zc[s, 0, c]
            field[s, c, 1 : total + 1, nz : nz + HALO, :] = zc[s, 1, c]
        for copy in copies:
            copy.wait_send()

    lane = lax.broadcasted_iota(jnp.int32, (8, ny), 1)
    mask_plus = (lane < ny - 1).astype(jnp.float32)
    mask_minus = (lane > 0).astype(jnp.float32)
    rows_y = lane[0:1].astype(jnp.float32) + 0.5
    wall = jnp.minimum(rows_y, ny - rows_y) / (ny / 2.0)

    def tendency(src, nu_s, r):
        around = [src.at[c, pl.ds(pl.multiple_of(r - 8, 8), 24), :] for c in range(3)]
        mid = [src[c, pl.ds(pl.multiple_of(r, 8), 8), :] for c in range(3)]
        visc = nu_s[pl.ds(pl.multiple_of(r, 8), 8), :]
        hu, hw, hv = mid[0] * 0.5, mid[1] * 0.5, mid[2] * 0.5
        x_plus, x_minus = visc - hu, visc + hu
        z_plus, z_minus = visc - hw, visc + hw
        y_plus, y_minus = (visc - hv) * mask_plus, (visc + hv) * mask_minus
        center = visc * -6.0
        out = []
        for c in range(3):
            value = center * mid[c]
            value += x_plus * src[c, pl.ds(pl.multiple_of(r + span, 8), 8), :]
            value += x_minus * src[c, pl.ds(pl.multiple_of(r - span, 8), 8), :]
            value += z_plus * around[c][9:17, :]
            value += z_minus * around[c][7:15, :]
            value += y_plus * pltpu.roll(mid[c], ny - 1, 1)
            value += y_minus * pltpu.roll(mid[c], 1, 1)
            if c == 0:
                value += DRIVE
            out.append(value)
        return mid, out

    def stages(s):
        v0 = field.at[s].reshape(4, rows, ny)
        v1 = field.at[s + 1].reshape(4, rows, ny)
        nu_s = nu.at[s].reshape(rows, ny)
        for k, (src, dst, scale) in enumerate(
            ((v0, w2, 0.5 * STEP), (w2, w3, 0.5 * STEP), (w3, w4, STEP)), 1
        ):

            def one(r, src=src, dst=dst, scale=scale):
                mid, out = tendency(src, nu_s, r)
                for c in range(3):
                    base = v0[c, pl.ds(pl.multiple_of(r, 8), 8), :]
                    dst[c, pl.ds(pl.multiple_of(r, 8), 8), :] = base + scale * out[c]

            def line(i, carry, k=k, one=one):
                start = k * span + nz + i * span
                for t in range(span // 8):
                    one(start + 8 * t)
                return carry

            total = nx + 2 * HALO
            lax.fori_loop(0, total - 2 * k, line, 0)
            one((total + 1 - k) * span - 8)

        def last(i, carry):
            start = (HALO + 1 + i) * span
            for t in range(nz // 8):
                r = start + 8 * t
                here = pl.ds(pl.multiple_of(r, 8), 8)
                mid, out = tendency(w4, nu_s, r)
                for c in range(3):
                    mean_part = (w2[c, here, :] + mid[c] - v0[c, here, :]) + 2.0 * w3[c, here, :]
                    v1[c, here, :] = mean_part * (1.0 / 3.0) + (STEP / 6.0) * out[c]
            return carry

        lax.fori_loop(0, nx, last, 0)

    def interior(s, c):
        return field[s, c, pl.ds(HALO + 1, nx), 0:nz, :]

    def start_gz(s):
        cells = nx * nz
        for c in range(3):
            value = interior(s + 1, c).reshape(cells, ny)
            part = jnp.dot(t1[...], value, precision=HIGH, preferred_element_type=jnp.float32)
            q_buf[s, :, c] = part.reshape(ngz, part.shape[0] // ngz, ny)

        def send(d, carry):
            pltpu.make_async_remote_copy(
                src_ref=q_buf.at[s, zpeer(d)],
                dst_ref=r_buf.at[s, d - 1],
                send_sem=gz_send.at[s],
                recv_sem=gz_recv.at[s],
                device_id=(gx, zpeer(d)),
                device_id_type=MESH,
            ).start()
            return carry

        lax.fori_loop(1, ngz, send, 0)
        r_buf[s, ngz - 1] = q_buf[s, gz]

    def wait_bytes(ref, sem):
        pltpu.make_async_copy(ref, ref, sem).wait()

    def start_gx(s):
        wait_bytes(r_buf.at[s, 0 : ngz - 1], gz_recv.at[s])
        p_flat = p_buf.at[s].reshape(ngx * 8, ny)
        for c in range(3):
            value = r_buf[s, :, c].reshape(t2.shape[1], ny)
            part = jnp.dot(t2[...], value, precision=HIGH, preferred_element_type=jnp.float32)
            for q in range(2):
                p_flat[pl.ds(2 * c + q, ngx, stride=8), :] = part[q * ngx : (q + 1) * ngx]
        for q in (6, 7):
            p_flat[pl.ds(q, ngx, stride=8), :] = jnp.zeros((ngx, ny), jnp.float32)

        def send(d, carry):
            pltpu.make_async_remote_copy(
                src_ref=p_buf.at[s, xpeer(d)],
                dst_ref=s_buf.at[s, d - 1],
                send_sem=gx_send.at[s],
                recv_sem=gx_recv.at[s],
                device_id=(xpeer(d), gz),
                device_id_type=MESH,
            ).start()
            return carry

        lax.fori_loop(1, ngx, send, 0)
        s_buf[s, ngx - 1] = p_buf[s, gx]

    def finish_gx(s):
        wait_bytes(s_buf.at[s, 0 : ngx - 1], gx_recv.at[s])
        coefs = jnp.sum(s_buf[s], axis=0)
        energy = jnp.sum(coefs * coefs) * (1.0 / ny)
        own = KZ // ngz
        wave = (gx // own) * KZ + gz * own + lax.rem(gx, own)
        energy = jnp.full((1, ny), energy, jnp.float32)
        goal = jnp.full((1, ny), target[wave], jnp.float32)
        ratio = (energy - goal) / (energy + goal)
        term[pl.ds(s, 1), :] = ratio * ratio

    def local_reward(s):
        offset = interior(s + 1, 0) - mean[...].reshape(1, 1, ny)
        square = offset * offset
        wide = jnp.concatenate([square[x] for x in range(nx)], axis=1)
        pick = (
            lax.broadcasted_iota(jnp.int32, (nx, nx * ny), 1) // ny
            == lax.broadcasted_iota(jnp.int32, (nx, nx * ny), 0)
        ).astype(jnp.float32)
        total = lax.dot_general(
            pick,
            wide,
            (((1,), (1,)), ((), ())),
            precision=HIGH,
            preferred_element_type=jnp.float32,
        )
        loc[s] = total * (-1.0 / ny)

    term[...] = jnp.zeros_like(term)
    load_vel.wait()
    pl.semaphore_wait(barrier, ngx + ngz + 2)
    start_halo(0, 4)
    load_t1.wait()
    load_t2.wait()
    wait_halo(0, 4)

    def viscosity(i, carry):
        each = field[0, 3, i]
        for s in range(steps):
            nu[s, i] = BASE_VISCOSITY + each[:, s : s + 1] * wall
        return carry

    lax.fori_loop(0, nx + 2 * HALO + 1, viscosity, 0)

    def body(s, carry):
        stages(s)

        @pl.when(s < steps - 1)
        def _():
            start_halo(s + 1, 3)

        start_gz(s)
        local_reward(s)

        @pl.when(s >= 1)
        def _():
            start_gx(s - 1)

        @pl.when(s >= 2)
        def _():
            finish_gx(s - 2)

        @pl.when(s < steps - 1)
        def _():
            wait_halo(s + 1, 3)

        return carry

    lax.fori_loop(0, steps, body, 0)

    store_vel = pltpu.make_async_copy(
        field.at[steps, 0:3, pl.ds(HALO + 1, nx), 0:nz, :], out_vel, local_sem.at[0]
    )
    store_vel.start()
    finish_gx(steps - 2)
    start_gx(steps - 1)

    plain = [None] * (past_steps + steps)
    running = boot[...]
    for t in range(past_steps + steps - 1, -1, -1):
        reward = past[t] if t < past_steps else loc[t - past_steps]
        running = reward + DISCOUNT * running
        plain[t] = running

    finish_gx(steps - 1)

    def send_x(d, carry):
        pltpu.make_async_remote_copy(
            src_ref=term,
            dst_ref=a_buf.at[d - 1],
            send_sem=ar_send.at[0],
            recv_sem=ar_recv.at[0],
            device_id=(xpeer(d), gz),
            device_id_type=MESH,
        ).start()
        return carry

    lax.fori_loop(1, ngx, send_x, 0)
    wait_bytes(a_buf, ar_recv.at[0])
    b_tile[...] = term[...] + jnp.sum(a_buf[...], axis=0)

    def send_z(d, carry):
        pltpu.make_async_remote_copy(
            src_ref=b_tile,
            dst_ref=b_buf.at[d - 1],
            send_sem=ar_send.at[1],
            recv_sem=ar_recv.at[1],
            device_id=(gx, zpeer(d)),
            device_id_type=MESH,
        ).start()
        return carry

    lax.fori_loop(1, ngz, send_z, 0)
    wait_bytes(b_buf, ar_recv.at[1])
    spectrum = (b_tile[...] + jnp.sum(b_buf[...], axis=0)) * (-1.0 / KX)

    extra = None
    for t in range(past_steps + steps - 1, -1, -1):
        if extra is not None:
            extra = extra * DISCOUNT
        if t >= past_steps:
            new = spectrum[t - past_steps : t - past_steps + 1, 0:nz]
            extra = new if extra is None else extra + new
        out_ret[t] = plain[t] + extra

    def drain(s, carry):
        wait_bytes(r_buf.at[s, 0 : ngz - 1], gz_send.at[s])
        wait_bytes(s_buf.at[s, 0 : ngx - 1], gx_send.at[s])
        return carry

    lax.fori_loop(0, steps, drain, 0)
    wait_bytes(a_buf, ar_send.at[0])
    wait_bytes(b_buf, ar_send.at[1])
    store_vel.wait()


def on_device(
    ngx, ngz, velocity, eddy_viscosity, target_spectrum, mean_profile, past_rewards, bootstrap_values
):
    nx, nz, ny = velocity.shape[1:]
    steps = eddy_viscosity.shape[0]
    horizon = past_rewards.shape[0] + steps
    t1 = z_table(ngz, nx, nz, nx * ngx, nz * ngz)
    t2 = x_table(ngx, ngz, nx, nx * ngx)
    span = nz + 2 * HALO
    lines = nx + 2 * HALO + 1
    f32 = jnp.float32
    vmem = pl.BlockSpec(memory_space=pltpu.VMEM)
    hbm = pl.BlockSpec(memory_space=pl.ANY)
    smem = pl.BlockSpec(memory_space=pltpu.SMEM)
    dma = pltpu.SemaphoreType.DMA
    return pl.pallas_call(
        functools.partial(kernel, ngx, ngz),
        out_shape=(
            jax.ShapeDtypeStruct(velocity.shape, f32),
            jax.ShapeDtypeStruct((horizon, nx, nz), f32),
        ),
        in_specs=[hbm, vmem, smem, vmem, vmem, vmem, hbm, hbm],
        out_specs=(hbm, vmem),
        scratch_shapes=[
            pltpu.VMEM((steps + 1, 4, lines, span, ny), f32),
            pltpu.VMEM((3, lines * span, ny), f32),
            pltpu.VMEM((3, lines * span, ny), f32),
            pltpu.VMEM((3, lines * span, ny), f32),
            pltpu.VMEM((steps, lines, span, ny), f32),
            pltpu.VMEM((steps, 2, 4, nx, HALO, ny), f32),
            pltpu.VMEM((steps, 2, 4, nx + 2 * HALO, HALO, ny), f32),
            pltpu.VMEM(t1.shape[1:], f32),
            pltpu.VMEM(t2.shape[1:], f32),
            pltpu.VMEM((steps, ngz, 3, t1.shape[1] // ngz, ny), f32),
            pltpu.VMEM((steps, ngz, 3, t1.shape[1] // ngz, ny), f32),
            pltpu.VMEM((steps, ngx, 8, ny), f32),
            pltpu.VMEM((steps, ngx, 8, ny), f32),
            pltpu.VMEM((steps, nx, nz), f32),
            pltpu.VMEM((8, ny), f32),
            pltpu.VMEM((ngx - 1, 8, ny), f32),
            pltpu.VMEM((8, ny), f32),
            pltpu.VMEM((ngz - 1, 8, ny), f32),
            dma((3,)),
            dma((steps, 8)),
            dma((steps, 8)),
            dma((steps,)),
            dma((steps,)),
            dma((steps,)),
            dma((steps,)),
            dma((2,)),
            dma((2,)),
        ],
        compiler_params=pltpu.CompilerParams(
            collective_id=0, has_side_effects=True, vmem_limit_bytes=48 * 1024 * 1024
        ),
        name="rollout",
    )(
        velocity,
        eddy_viscosity,
        target_spectrum,
        mean_profile.reshape(1, ny),
        past_rewards,
        bootstrap_values,
        jnp.asarray(t1),
        jnp.asarray(t2),
    )


def solution(mesh):
    placed = (
        P(None, "gx", "gz", None),
        P(None, "gx", "gz"),
        P(),
        P(),
        P(None, "gx", "gz"),
        P("gx", "gz"),
    )
    return jax.shard_map(
        functools.partial(on_device, mesh.shape["gx"], mesh.shape["gz"]),
        mesh=mesh,
        in_specs=placed,
        out_specs=(P(None, "gx", "gz", None), P(None, "gx", "gz")),
        check_vma=False,
    )
```

```python
import functools
import math

import numpy as np

import jax
import jax.numpy as jnp
from jax import lax
from jax.experimental import pallas as pl
from jax.experimental.pallas import tpu as pltpu
from jax.sharding import PartitionSpec as P

KX = 16
KZ = 16
STEP = 0.05
BASE_VISCOSITY = 0.02
DRIVE = 0.5
DISCOUNT = 0.97
HALO = 4
MESH = pl.DeviceIdType.MESH
HIGH = lax.Precision.HIGHEST


def z_table(peers, cells_x, cells_z, total_x, total_z):
    own = KZ // peers
    factor = 1.0 / math.sqrt(total_x * total_z)
    spots = np.arange(peers)[:, None] * cells_z + np.arange(cells_z)[None, :]
    turns = (np.arange(KZ)[None, :, None] * spots[:, None, :]) % total_z
    angle = turns * (2.0 * math.pi / total_z)
    waves = np.stack([np.cos(angle), -np.sin(angle)], axis=2) * factor
    eye = np.eye(cells_x)
    table = np.einsum("gkrz,ab->gkraBz".replace("B", "b"), waves, eye)
    rows = peers * own * 2 * cells_x
    return table.reshape(peers, rows, cells_x * cells_z).astype(np.float32)


def x_table(devices, peers, cells_x, total_x):
    own = KZ // peers
    spots = np.arange(devices)[:, None] * cells_x + np.arange(cells_x)[None, :]
    turns = (np.arange(KX)[None, :, None] * spots[:, None, :]) % total_x
    angle = turns * (2.0 * math.pi / total_x)
    c, s = np.cos(angle), np.sin(angle)
    spin = np.stack([np.stack([c, s], 2), np.stack([-s, c], 2)], 1)
    eye = np.eye(own)
    table = np.einsum("gqkrx,ab->gqkabrx", spin, eye)
    table = table.reshape(devices, 2 * KX * own, 1, own * 2 * cells_x)
    table = np.broadcast_to(table, (devices, 2 * KX * own, peers, own * 2 * cells_x))
    return table.reshape(devices, 2 * KX * own, peers * own * 2 * cells_x).astype(np.float32)


def kernel(
    ngx,
    ngz,
    vel,
    eddy_hbm,
    target,
    mean_hbm,
    past_hbm,
    boot_hbm,
    t1_hbm,
    t2_hbm,
    out_vel,
    out_hbm,
    eddy,
    mean,
    past,
    boot,
    out_ret,
    fresh,
    field,
    w2,
    w3,
    w4,
    nu,
    pack,
    zc,
    corner_out,
    corner_in,
    t1,
    t2,
    q_buf,
    r_buf,
    p_buf,
    s_buf,
    loc,
    term,
    a_buf,
    b_tile,
    b_buf,
    local_sem,
    halo_send,
    halo_recv,
    gz_send,
    gz_recv,
    gx_send,
    gx_recv,
    ar_send,
    ar_recv,
):
    gx = lax.axis_index("gx")
    gz = lax.axis_index("gz")
    steps = eddy.shape[0]
    nx = vel.shape[1]
    nz = vel.shape[2]
    ny = vel.shape[3]
    span = nz + 2 * HALO
    rows = (nx + 2 * HALO + 3) * span
    past_steps = past.shape[0]

    def each_far(count, send):
        for step in range(count - 1):
            away = (step + 1) // 2
            send(count // 2 + (away if step % 2 else -away), 0)

    def xpeer(d):
        return lax.rem(gx + d + ngx, ngx)

    def zpeer(d):
        return lax.rem(gz + d + ngz, ngz)

    load_vel = pltpu.make_async_copy(
        vel, field.at[0, 0:3, pl.ds(HALO + 1, nx), 0:nz, :], local_sem.at[0]
    )
    load_t1 = pltpu.make_async_copy(t1_hbm.at[gz], t1, local_sem.at[1])
    load_t2 = pltpu.make_async_copy(t2_hbm.at[gx], t2, local_sem.at[2])
    load_eddy = pltpu.make_async_copy(eddy_hbm, eddy, local_sem.at[3])
    load_mean = pltpu.make_async_copy(mean_hbm, mean, local_sem.at[4])
    load_past = pltpu.make_async_copy(past_hbm, past, local_sem.at[5])
    load_boot = pltpu.make_async_copy(boot_hbm, boot, local_sem.at[6])
    load_eddy.start()
    load_vel.start()
    for load in (load_t1, load_t2, load_mean, load_past, load_boot):
        load.start()

    barrier = pltpu.get_barrier_semaphore()

    def greet_x(d, carry):
        pl.semaphore_signal(barrier, inc=1, device_id=(xpeer(d), gz), device_id_type=MESH)
        return carry

    def greet_z(d, carry):
        pl.semaphore_signal(barrier, inc=1, device_id=(gx, zpeer(d)), device_id_type=MESH)
        return carry

    lax.fori_loop(1, ngx, greet_x, 0)
    lax.fori_loop(1, ngz, greet_z, 0)
    for dx in (-1, 1):
        for dz in (-1, 1):
            pl.semaphore_signal(
                barrier, inc=1, device_id=(xpeer(dx), zpeer(dz)), device_id_type=MESH
            )

    load_eddy.wait()
    eye = (
        lax.broadcasted_iota(jnp.int32, (steps, ny), 0)
        == lax.broadcasted_iota(jnp.int32, (steps, ny), 1)
    ).astype(jnp.float32)
    for x in range(nx):
        field[0, 3, HALO + 1 + x, 0:nz, :] = lax.dot_general(
            eddy[:, x, :],
            eye,
            (((0,), (0,)), ((), ())),
            precision=HIGH,
            preferred_element_type=jnp.float32,
        )

    first = HALO + 1
    corners = [(dx, dz) for dx in (1, -1) for dz in (1, -1)]

    def halo_copies(s, comps):
        copies = []
        for index, (dx, dz) in enumerate(corners):
            copies.append((corner_out.at[s, index, 0:comps], corner_in.at[s, index, 0:comps], dx, dz))
        for side, dz in ((0, 1), (1, -1)):
            copies.append((pack.at[s, side, 0:comps], zc.at[s, side, 0:comps], 0, dz))
        for dx, src, dst in ((1, first + nx - HALO, 1), (-1, first, first + nx)):
            copies.append(
                (
                    field.at[s, 0:comps, pl.ds(src, HALO), 0:nz, :],
                    field.at[s, 0:comps, pl.ds(dst, HALO), 0:nz, :],
                    dx,
                    0,
                )
            )
        return [
            pltpu.make_async_remote_copy(
                src_ref=src,
                dst_ref=dst,
                send_sem=halo_send.at[s, index],
                recv_sem=halo_recv.at[s, index],
                device_id=(xpeer(dx), zpeer(dz)),
                device_id_type=MESH,
            )
            for index, (src, dst, dx, dz) in enumerate(copies)
        ]

    diamond = []
    taken = 0
    for away in range(1, HALO):
        diamond.append((away, taken, HALO - away))
        taken += HALO - away

    def start_halo(s, comps):
        for index, (dx, dz) in enumerate(corners):
            for c in range(comps):
                for away, at, count in diamond:
                    line = first + nx - away if dx == 1 else first + away - 1
                    head = nz - count if dz == 1 else 0
                    corner_out[s, index, c, at : at + count, :] = field[
                        s, c, line, head : head + count, :
                    ]
        for c in range(comps):
            pack[s, 0, c] = field[s, c, pl.ds(first, nx), nz - HALO : nz, :]
            pack[s, 1, c] = field[s, c, pl.ds(first, nx), 0:HALO, :]
        for copy in halo_copies(s, comps):
            copy.start()

    def wait_halo(s, comps):
        copies = halo_copies(s, comps)
        for copy in copies:
            copy.wait_recv()
        for c in range(comps):
            field[s, c, pl.ds(first - 1, nx), nz + HALO : span, :] = zc[s, 0, c]
            field[s, c, pl.ds(first, nx), nz : nz + HALO, :] = zc[s, 1, c]
        for index, (dx, dz) in enumerate(corners):
            for c in range(comps):
                for away, at, count in diamond:
                    line = first - away if dx == 1 else first + nx - 1 + away
                    if dz == 1:
                        line, head = line - 1, span - count
                    else:
                        head = nz
                    field[s, c, line, head : head + count, :] = corner_in[
                        s, index, c, at : at + count, :
                    ]
        for copy in copies:
            copy.wait_send()

    lane = lax.broadcasted_iota(jnp.int32, (8, ny), 1)
    mask_plus = (lane < ny - 1).astype(jnp.float32)
    mask_minus = (lane > 0).astype(jnp.float32)
    rows_y = lane[0:1].astype(jnp.float32) + 0.5
    wall = jnp.minimum(rows_y, ny - rows_y) / (ny / 2.0)

    def here(r):
        return pl.ds(pl.multiple_of(r, 8), 8)

    def advance(src, nu_s, r, scale, base):
        mid = [src[c, here(r), :] for c in range(3)]
        visc = nu_s[here(r), :] * scale
        half = 0.5 * scale
        hu, hw, hv = mid[0] * half, mid[1] * half, mid[2] * half
        x_plus, x_minus = visc - hu, visc + hu
        z_plus, z_minus = visc - hw, visc + hw
        y_plus, y_minus = (visc - hv) * mask_plus, (visc + hv) * mask_minus
        center = visc * -6.0
        if base is None:
            center = center + 1.0
        out = []
        for c in range(3):
            around = src.at[c, pl.ds(pl.multiple_of(r - 8, 8), 24), :]
            value = center * mid[c]
            if base is not None:
                value += base(c, mid[c])
            if c == 0:
                value += DRIVE * scale
            value += x_plus * src[c, here(r + span), :]
            value += x_minus * src[c, here(r - span), :]
            value += z_plus * around[9:17, :]
            value += z_minus * around[7:15, :]
            value += y_plus * pltpu.roll(mid[c], ny - 1, 1)
            value += y_minus * pltpu.roll(mid[c], 1, 1)
            out.append(value)
        return out

    def stages(s):
        v0 = field.at[s].reshape(4, rows, ny)
        nu_s = nu.at[s].reshape(rows, ny)
        total = nx + 2 * HALO

        def start_value(r):
            return lambda c, mid: v0[c, here(r), :]

        def last_value(r):
            return lambda c, mid: (
                (w2[c, here(r), :] + mid - v0[c, here(r), :]) + 2.0 * w3[c, here(r), :]
            ) * (1.0 / 3.0)

        plan = (
            (v0, w2, 0.5 * STEP, lambda r: None),
            (w2, w3, 0.5 * STEP, start_value),
            (w3, w4, STEP, start_value),
            (w4, fresh, STEP / 6.0, last_value),
        )
        for k, (src, dst, scale, base) in enumerate(plan, 1):
            final = k == len(plan)
            head = k * span + nz + (span - nz if final else 0)
            tiles = (nz if final else span) // 8

            def one(r, src=src, dst=dst, scale=scale, base=base):
                out = advance(src, nu_s, r, scale, base(r))
                for c in range(3):
                    dst[c, here(r), :] = out[c]

            def line(i, carry, one=one, head=head, tiles=tiles):
                def tile(t, inner):
                    one(head + i * span + 8 * t)
                    return inner

                return lax.fori_loop(0, tiles, tile, carry, unroll=True)

            lax.fori_loop(0, total - 2 * k, line, 0, unroll=True)
            if not final:
                one((total + 1 - k) * span - 8)
        for c in range(3):
            for x in range(nx):
                field[s + 1, c, first + x, 0:nz, :] = fresh[c, pl.ds((first + x) * span, nz), :]

    def interior(s, c):
        return field[s, c, pl.ds(HALO + 1, nx), 0:nz, :]

    def start_gz(s):
        cells = nx * nz
        for c in range(3):
            value = interior(s + 1, c).reshape(cells, ny)
            part = jnp.dot(t1[...], value, precision=HIGH, preferred_element_type=jnp.float32)
            q_buf[s, :, c] = part.reshape(ngz, part.shape[0] // ngz, ny)

        def send(d, carry):
            pltpu.make_async_remote_copy(
                src_ref=q_buf.at[s, zpeer(d)],
                dst_ref=r_buf.at[s, d - 1],
                send_sem=gz_send.at[s],
                recv_sem=gz_recv.at[s],
                device_id=(gx, zpeer(d)),
                device_id_type=MESH,
            ).start()
            return carry

        each_far(ngz, send)
        r_buf[s, ngz - 1] = q_buf[s, gz]

    def wait_bytes(ref, sem):
        pltpu.make_async_copy(ref, ref, sem).wait()

    def start_gx(s):
        wait_bytes(r_buf.at[s, 0 : ngz - 1], gz_recv.at[s])
        p_flat = p_buf.at[s].reshape(ngx * 8, ny)
        for c in range(3):
            value = r_buf[s, :, c].reshape(t2.shape[1], ny)
            part = jnp.dot(t2[...], value, precision=HIGH, preferred_element_type=jnp.float32)
            for q in range(2):
                p_flat[pl.ds(2 * c + q, ngx, stride=8), :] = part[q * ngx : (q + 1) * ngx]
        for q in (6, 7):
            p_flat[pl.ds(q, ngx, stride=8), :] = jnp.zeros((ngx, ny), jnp.float32)

        def send(d, carry):
            pltpu.make_async_remote_copy(
                src_ref=p_buf.at[s, xpeer(d)],
                dst_ref=s_buf.at[s, d - 1],
                send_sem=gx_send.at[s],
                recv_sem=gx_recv.at[s],
                device_id=(xpeer(d), gz),
                device_id_type=MESH,
            ).start()
            return carry

        each_far(ngx, send)
        s_buf[s, ngx - 1] = p_buf[s, gx]

    def finish_gx(s):
        wait_bytes(s_buf.at[s, 0 : ngx - 1], gx_recv.at[s])
        coefs = jnp.sum(s_buf[s], axis=0)
        energy = jnp.sum(coefs * coefs) * (1.0 / ny)
        own = KZ // ngz
        wave = (gx // own) * KZ + gz * own + lax.rem(gx, own)
        energy = jnp.full((1, ny), energy, jnp.float32)
        goal = jnp.full((1, ny), target[wave], jnp.float32)
        ratio = (energy - goal) / (energy + goal)
        term[pl.ds(s, 1), :] = ratio * ratio

    def local_reward(s):
        offset = interior(s + 1, 0) - mean[...].reshape(1, 1, ny)
        square = offset * offset
        wide = jnp.concatenate([square[x] for x in range(nx)], axis=1)
        pick = (
            lax.broadcasted_iota(jnp.int32, (nx, nx * ny), 1) // ny
            == lax.broadcasted_iota(jnp.int32, (nx, nx * ny), 0)
        ).astype(jnp.float32)
        total = lax.dot_general(
            pick,
            wide,
            (((1,), (1,)), ((), ())),
            precision=HIGH,
            preferred_element_type=jnp.float32,
        )
        loc[s] = total * (-1.0 / ny)

    term[...] = jnp.zeros_like(term)
    load_vel.wait()
    pl.semaphore_wait(barrier, ngx + ngz + 2)
    start_halo(0, 4)
    for load in (load_t1, load_t2, load_mean, load_past, load_boot):
        load.wait()
    wait_halo(0, 4)

    def viscosity(s):
        def each(i, carry):
            nu[s, i] = BASE_VISCOSITY + field[0, 3, i][:, s : s + 1] * wall
            return carry

        lax.fori_loop(0, nx + 2 * HALO + 1, each, 0)

    viscosity(0)

    def body(s, carry):
        stages(s)

        @pl.when(s < steps - 1)
        def _():
            start_halo(s + 1, 3)

        start_gz(s)
        local_reward(s)
        for later in range(1, steps):
            pl.when(s == later - 1)(functools.partial(viscosity, later))

        @pl.when(s >= 1)
        def _():
            start_gx(s - 1)

        @pl.when(s >= 2)
        def _():
            finish_gx(s - 2)

        @pl.when(s < steps - 1)
        def _():
            wait_halo(s + 1, 3)

        return carry

    lax.fori_loop(0, steps, body, 0)

    store_vel = pltpu.make_async_copy(
        field.at[steps, 0:3, pl.ds(HALO + 1, nx), 0:nz, :], out_vel, local_sem.at[0]
    )
    store_vel.start()
    finish_gx(steps - 2)
    start_gx(steps - 1)

    plain = [None] * (past_steps + steps)
    running = boot[...]
    for t in range(past_steps + steps - 1, -1, -1):
        reward = past[t] if t < past_steps else loc[t - past_steps]
        running = reward + DISCOUNT * running
        plain[t] = running

    finish_gx(steps - 1)

    def send_x(d, carry):
        pltpu.make_async_remote_copy(
            src_ref=term,
            dst_ref=a_buf.at[d - 1],
            send_sem=ar_send.at[0],
            recv_sem=ar_recv.at[0],
            device_id=(xpeer(d), gz),
            device_id_type=MESH,
        ).start()
        return carry

    each_far(ngx, send_x)
    wait_bytes(a_buf, ar_recv.at[0])
    b_tile[...] = term[...] + jnp.sum(a_buf[...], axis=0)

    def send_z(d, carry):
        pltpu.make_async_remote_copy(
            src_ref=b_tile,
            dst_ref=b_buf.at[d - 1],
            send_sem=ar_send.at[1],
            recv_sem=ar_recv.at[1],
            device_id=(gx, zpeer(d)),
            device_id_type=MESH,
        ).start()
        return carry

    each_far(ngz, send_z)
    wait_bytes(b_buf, ar_recv.at[1])
    spectrum = (b_tile[...] + jnp.sum(b_buf[...], axis=0)) * (-1.0 / KX)

    extra = None
    for t in range(past_steps + steps - 1, -1, -1):
        if extra is not None:
            extra = extra * DISCOUNT
        if t >= past_steps:
            new = spectrum[t - past_steps : t - past_steps + 1, 0:nz]
            extra = new if extra is None else extra + new
        out_ret[t] = plain[t] + extra
    store_ret = pltpu.make_async_copy(out_ret, out_hbm, local_sem.at[1])
    store_ret.start()

    def drain(s, carry):
        wait_bytes(r_buf.at[s, 0 : ngz - 1], gz_send.at[s])
        wait_bytes(s_buf.at[s, 0 : ngx - 1], gx_send.at[s])
        return carry

    lax.fori_loop(0, steps, drain, 0)
    wait_bytes(a_buf, ar_send.at[0])
    wait_bytes(b_buf, ar_send.at[1])
    store_vel.wait()
    store_ret.wait()


def place(vel, ret, out_vel, out_ret):
    out_vel[...] = vel[...]
    out_ret[...] = ret[...]


def on_device(
    ngx, ngz, velocity, eddy_viscosity, target_spectrum, mean_profile, past_rewards, bootstrap_values
):
    nx, nz, ny = velocity.shape[1:]
    steps = eddy_viscosity.shape[0]
    horizon = past_rewards.shape[0] + steps
    t1 = z_table(ngz, nx, nz, nx * ngx, nz * ngz)
    t2 = x_table(ngx, ngz, nx, nx * ngx)
    span = nz + 2 * HALO
    lines = nx + 2 * HALO + 3
    f32 = jnp.float32
    hbm = pl.BlockSpec(memory_space=pltpu.HBM)
    free = pl.BlockSpec(memory_space=pl.ANY)
    smem = pl.BlockSpec(memory_space=pltpu.SMEM)
    dma = pltpu.SemaphoreType.DMA
    found = pl.pallas_call(
        functools.partial(kernel, ngx, ngz),
        out_shape=(
            jax.ShapeDtypeStruct(velocity.shape, f32),
            jax.ShapeDtypeStruct((horizon, nx, nz), f32),
        ),
        in_specs=[hbm, hbm, smem, hbm, hbm, hbm, hbm, hbm],
        out_specs=(free, free),
        scratch_shapes=[
            pltpu.VMEM(eddy_viscosity.shape, f32),
            pltpu.VMEM((1, ny), f32),
            pltpu.VMEM(past_rewards.shape, f32),
            pltpu.VMEM(bootstrap_values.shape, f32),
            pltpu.VMEM((horizon, nx, nz), f32),
            pltpu.VMEM((3, lines * span, ny), f32),
            pltpu.VMEM((steps + 1, 4, lines, span, ny), f32),
            pltpu.VMEM((3, lines * span, ny), f32),
            pltpu.VMEM((3, lines * span, ny), f32),
            pltpu.VMEM((3, lines * span, ny), f32),
            pltpu.VMEM((steps, lines, span, ny), f32),
            pltpu.VMEM((steps, 2, 4, nx, HALO, ny), f32),
            pltpu.VMEM((steps, 2, 4, nx, HALO, ny), f32),
            pltpu.VMEM((steps, 4, 4, 8, ny), f32),
            pltpu.VMEM((steps, 4, 4, 8, ny), f32),
            pltpu.VMEM(t1.shape[1:], f32),
            pltpu.VMEM(t2.shape[1:], f32),
            pltpu.VMEM((steps, ngz, 3, t1.shape[1] // ngz, ny), f32),
            pltpu.VMEM((steps, ngz, 3, t1.shape[1] // ngz, ny), f32),
            pltpu.VMEM((steps, ngx, 8, ny), f32),
            pltpu.VMEM((steps, ngx, 8, ny), f32),
            pltpu.VMEM((steps, nx, nz), f32),
            pltpu.VMEM((8, ny), f32),
            pltpu.VMEM((ngx - 1, 8, ny), f32),
            pltpu.VMEM((8, ny), f32),
            pltpu.VMEM((ngz - 1, 8, ny), f32),
            dma((7,)),
            dma((steps, 8)),
            dma((steps, 8)),
            dma((steps,)),
            dma((steps,)),
            dma((steps,)),
            dma((steps,)),
            dma((2,)),
            dma((2,)),
        ],
        compiler_params=pltpu.CompilerParams(
            collective_id=0, has_side_effects=True, vmem_limit_bytes=62 * 1024 * 1024
        ),
        name="rollout",
    )(
        velocity,
        eddy_viscosity,
        target_spectrum,
        mean_profile.reshape(1, ny),
        past_rewards,
        bootstrap_values,
        jnp.asarray(t1),
        jnp.asarray(t2),
    )

    return pl.pallas_call(
        place,
        out_shape=tuple(jax.ShapeDtypeStruct(part.shape, f32) for part in found),
        in_specs=[pl.BlockSpec(memory_space=pltpu.VMEM)] * 2,
        out_specs=(pl.BlockSpec(memory_space=pltpu.VMEM),) * 2,
        name="place",
    )(*found)


def solution(mesh):
    placed = (
        P(None, "gx", "gz", None),
        P(None, "gx", "gz"),
        P(),
        P(),
        P(None, "gx", "gz"),
        P("gx", "gz"),
    )
    return jax.shard_map(
        functools.partial(on_device, mesh.shape["gx"], mesh.shape["gz"]),
        mesh=mesh,
        in_specs=placed,
        out_specs=(P(None, "gx", "gz", None), P(None, "gx", "gz")),
        check_vma=False,
    )
```

```python
import functools
import math

import numpy as np

import jax
import jax.numpy as jnp
from jax import lax
from jax.experimental import pallas as pl
from jax.experimental.pallas import tpu as pltpu
from jax.sharding import PartitionSpec as P

KX = 16
KZ = 16
STEP = 0.05
BASE_VISCOSITY = 0.02
DRIVE = 0.5
DISCOUNT = 0.97
HALO = 4
MESH = pl.DeviceIdType.MESH
HIGH = lax.Precision.HIGHEST


def z_table(peers, cells_x, cells_z, total_x, total_z):
    own = KZ // peers
    factor = 1.0 / math.sqrt(total_x * total_z)
    spots = np.arange(peers)[:, None] * cells_z + np.arange(cells_z)[None, :]
    turns = (np.arange(KZ)[None, :, None] * spots[:, None, :]) % total_z
    angle = turns * (2.0 * math.pi / total_z)
    waves = np.stack([np.cos(angle), -np.sin(angle)], axis=2) * factor
    eye = np.eye(cells_x)
    table = np.einsum("gkrz,ab->gkraBz".replace("B", "b"), waves, eye)
    rows = peers * own * 2 * cells_x
    return table.reshape(peers, rows, cells_x * cells_z).astype(np.float32)


def x_table(devices, peers, cells_x, total_x):
    own = KZ // peers
    spots = np.arange(devices)[:, None] * cells_x + np.arange(cells_x)[None, :]
    turns = (np.arange(KX)[None, :, None] * spots[:, None, :]) % total_x
    angle = turns * (2.0 * math.pi / total_x)
    c, s = np.cos(angle), np.sin(angle)
    spin = np.stack([np.stack([c, s], 2), np.stack([-s, c], 2)], 1)
    eye = np.eye(own)
    table = np.einsum("gqkrx,ab->gqkabrx", spin, eye)
    table = table.reshape(devices, 2 * KX * own, 1, own * 2 * cells_x)
    table = np.broadcast_to(table, (devices, 2 * KX * own, peers, own * 2 * cells_x))
    return table.reshape(devices, 2 * KX * own, peers * own * 2 * cells_x).astype(np.float32)


def kernel(
    ngx,
    ngz,
    vel,
    eddy_hbm,
    target,
    mean_hbm,
    past_hbm,
    boot_hbm,
    t1_hbm,
    t2_hbm,
    out_vel,
    out_hbm,
    eddy,
    mean,
    past,
    boot,
    out_ret,
    fresh,
    field,
    w2,
    w3,
    w4,
    nu,
    pack,
    zc,
    corner_out,
    corner_in,
    t1,
    t2,
    q_buf,
    r_buf,
    p_buf,
    s_buf,
    loc,
    term,
    a_buf,
    b_tile,
    b_buf,
    local_sem,
    halo_send,
    halo_recv,
    gz_send,
    gz_recv,
    gx_send,
    gx_recv,
    ar_send,
    ar_recv,
):
    gx = lax.axis_index("gx")
    gz = lax.axis_index("gz")
    steps = eddy.shape[0]
    nx = vel.shape[1]
    nz = vel.shape[2]
    ny = vel.shape[3]
    span = nz + 2 * HALO
    rows = (nx + 2 * HALO + 3) * span
    past_steps = past.shape[0]

    def each_far(count, send):
        for step in range(count - 1):
            away = (step + 1) // 2
            send(count // 2 + (away if step % 2 else -away), 0)

    def xpeer(d):
        return lax.rem(gx + d + ngx, ngx)

    def zpeer(d):
        return lax.rem(gz + d + ngz, ngz)

    load_vel = pltpu.make_async_copy(
        vel, field.at[0, 0:3, pl.ds(HALO + 1, nx), 0:nz, :], local_sem.at[0]
    )
    load_t1 = pltpu.make_async_copy(t1_hbm.at[gz], t1, local_sem.at[1])
    load_t2 = pltpu.make_async_copy(t2_hbm.at[gx], t2, local_sem.at[2])
    load_eddy = pltpu.make_async_copy(eddy_hbm, eddy, local_sem.at[3])
    load_mean = pltpu.make_async_copy(mean_hbm, mean, local_sem.at[4])
    load_past = pltpu.make_async_copy(past_hbm, past, local_sem.at[5])
    load_boot = pltpu.make_async_copy(boot_hbm, boot, local_sem.at[6])
    load_eddy.start()
    load_vel.start()
    for load in (load_t1, load_t2, load_mean, load_past, load_boot):
        load.start()

    barrier = pltpu.get_barrier_semaphore()

    def greet_x(d, carry):
        pl.semaphore_signal(barrier, inc=1, device_id=(xpeer(d), gz), device_id_type=MESH)
        return carry

    def greet_z(d, carry):
        pl.semaphore_signal(barrier, inc=1, device_id=(gx, zpeer(d)), device_id_type=MESH)
        return carry

    lax.fori_loop(1, ngx, greet_x, 0)
    lax.fori_loop(1, ngz, greet_z, 0)
    for dx in (-1, 1):
        for dz in (-1, 1):
            pl.semaphore_signal(
                barrier, inc=1, device_id=(xpeer(dx), zpeer(dz)), device_id_type=MESH
            )

    load_eddy.wait()
    eye = (
        lax.broadcasted_iota(jnp.int32, (steps, ny), 0)
        == lax.broadcasted_iota(jnp.int32, (steps, ny), 1)
    ).astype(jnp.float32)
    for x in range(nx):
        field[0, 3, HALO + 1 + x, 0:nz, :] = lax.dot_general(
            eddy[:, x, :],
            eye,
            (((0,), (0,)), ((), ())),
            precision=HIGH,
            preferred_element_type=jnp.float32,
        )

    first = HALO + 1
    corners = [(dx, dz) for dx in (1, -1) for dz in (1, -1)]

    def halo_copies(s, comps):
        copies = []
        for index, (dx, dz) in enumerate(corners):
            copies.append((corner_out.at[s, index, 0:comps], corner_in.at[s, index, 0:comps], dx, dz))
        for side, dz in ((0, 1), (1, -1)):
            copies.append((pack.at[s, side, 0:comps], zc.at[s, side, 0:comps], 0, dz))
        for dx, src, dst in ((1, first + nx - HALO, 1), (-1, first, first + nx)):
            copies.append(
                (
                    field.at[s, 0:comps, pl.ds(src, HALO), 0:nz, :],
                    field.at[s, 0:comps, pl.ds(dst, HALO), 0:nz, :],
                    dx,
                    0,
                )
            )
        return [
            pltpu.make_async_remote_copy(
                src_ref=src,
                dst_ref=dst,
                send_sem=halo_send.at[s, index],
                recv_sem=halo_recv.at[s, index],
                device_id=(xpeer(dx), zpeer(dz)),
                device_id_type=MESH,
            )
            for index, (src, dst, dx, dz) in enumerate(copies)
        ]

    diamond = []
    taken = 0
    for away in range(1, HALO):
        diamond.append((away, taken, HALO - away))
        taken += HALO - away

    def start_halo(s, comps):
        for index, (dx, dz) in enumerate(corners):
            for c in range(comps):
                for away, at, count in diamond:
                    line = first + nx - away if dx == 1 else first + away - 1
                    head = nz - count if dz == 1 else 0
                    corner_out[s, index, c, at : at + count, :] = field[
                        s, c, line, head : head + count, :
                    ]
        for c in range(comps):
            pack[s, 0, c] = field[s, c, pl.ds(first, nx), nz - HALO : nz, :]
            pack[s, 1, c] = field[s, c, pl.ds(first, nx), 0:HALO, :]
        for copy in halo_copies(s, comps):
            copy.start()

    def wait_x(s, comps):
        for copy in halo_copies(s, comps)[6:]:
            copy.wait_recv()

    def wait_z(s, comps):
        for copy in halo_copies(s, comps)[:6]:
            copy.wait_recv()
        for c in range(comps):
            field[s, c, pl.ds(first - 1, nx), nz + HALO : span, :] = zc[s, 0, c]
            field[s, c, pl.ds(first, nx), nz : nz + HALO, :] = zc[s, 1, c]
        for index, (dx, dz) in enumerate(corners):
            for c in range(comps):
                for away, at, count in diamond:
                    line = first - away if dx == 1 else first + nx - 1 + away
                    if dz == 1:
                        line, head = line - 1, span - count
                    else:
                        head = nz
                    field[s, c, line, head : head + count, :] = corner_in[
                        s, index, c, at : at + count, :
                    ]

    def wait_sent(s, comps):
        for copy in halo_copies(s, comps):
            copy.wait_send()

    lane = lax.broadcasted_iota(jnp.int32, (8, ny), 1)
    mask_plus = (lane < ny - 1).astype(jnp.float32)
    mask_minus = (lane > 0).astype(jnp.float32)
    rows_y = lane[0:1].astype(jnp.float32) + 0.5
    wall = jnp.minimum(rows_y, ny - rows_y) / (ny / 2.0)

    def here(r):
        return pl.ds(pl.multiple_of(r, 8), 8)

    def advance(src, nu_s, r, scale, base):
        mid = [src[c, here(r), :] for c in range(3)]
        visc = nu_s[here(r), :] * scale
        half = 0.5 * scale
        hu, hw, hv = mid[0] * half, mid[1] * half, mid[2] * half
        x_plus, x_minus = visc - hu, visc + hu
        z_plus, z_minus = visc - hw, visc + hw
        y_plus, y_minus = (visc - hv) * mask_plus, (visc + hv) * mask_minus
        center = visc * -6.0
        if base is None:
            center = center + 1.0
        out = []
        for c in range(3):
            around = src.at[c, pl.ds(pl.multiple_of(r - 8, 8), 24), :]
            value = center * mid[c]
            if base is not None:
                value += base(c, mid[c])
            if c == 0:
                value += DRIVE * scale
            value += x_plus * src[c, here(r + span), :]
            value += x_minus * src[c, here(r - span), :]
            value += z_plus * around[9:17, :]
            value += z_minus * around[7:15, :]
            value += y_plus * pltpu.roll(mid[c], ny - 1, 1)
            value += y_minus * pltpu.roll(mid[c], 1, 1)
            out.append(value)
        return out

    def stages(s, inner):
        v0 = field.at[s].reshape(4, rows, ny)
        nu_s = nu.at[s].reshape(rows, ny)
        total = nx + 2 * HALO

        def start_value(r):
            return lambda c, mid: v0[c, here(r), :]

        def last_value(r):
            return lambda c, mid: (
                (w2[c, here(r), :] + mid - v0[c, here(r), :]) + 2.0 * w3[c, here(r), :]
            ) * (1.0 / 3.0)

        plan = (
            (v0, w2, 0.5 * STEP, lambda r: None),
            (w2, w3, 0.5 * STEP, start_value),
            (w3, w4, STEP, start_value),
            (w4, fresh, STEP / 6.0, last_value),
        )
        for k, (src, dst, scale, base) in enumerate(plan, 1):
            final = k == len(plan)
            if inner:
                tiles = range(8, nz - 8, 8) if final else range(0, nz, 8)
            else:
                tiles = (0, nz - 8) if final else (-8, 0, nz - 8)

            def one(r, src=src, dst=dst, scale=scale, base=base):
                out = advance(src, nu_s, r, scale, base(r))
                for c in range(3):
                    dst[c, here(r), :] = out[c]

            def line(i, carry, k=k, one=one, tiles=tiles):
                for t in tiles:
                    one((k + 1 + i) * span + t)
                return carry

            lax.fori_loop(0, total - 2 * k, line, 0, unroll=True)
            if not inner and not final:
                one((total + 1 - k) * span - 8)

    def settle(s):
        for c in range(3):
            for x in range(nx):
                field[s + 1, c, first + x, 0:nz, :] = fresh[c, pl.ds((first + x) * span, nz), :]

    def interior(s, c):
        return field[s, c, pl.ds(HALO + 1, nx), 0:nz, :]

    def start_gz(s):
        cells = nx * nz
        for c in range(3):
            value = interior(s + 1, c).reshape(cells, ny)
            part = jnp.dot(t1[...], value, precision=HIGH, preferred_element_type=jnp.float32)
            q_buf[s, :, c] = part.reshape(ngz, part.shape[0] // ngz, ny)

        def send(d, carry):
            pltpu.make_async_remote_copy(
                src_ref=q_buf.at[s, zpeer(d)],
                dst_ref=r_buf.at[s, d - 1],
                send_sem=gz_send.at[s],
                recv_sem=gz_recv.at[s],
                device_id=(gx, zpeer(d)),
                device_id_type=MESH,
            ).start()
            return carry

        each_far(ngz, send)
        r_buf[s, ngz - 1] = q_buf[s, gz]

    def wait_bytes(ref, sem):
        pltpu.make_async_copy(ref, ref, sem).wait()

    def start_gx(s):
        wait_bytes(r_buf.at[s, 0 : ngz - 1], gz_recv.at[s])
        p_flat = p_buf.at[s].reshape(ngx * 8, ny)
        for c in range(3):
            value = r_buf[s, :, c].reshape(t2.shape[1], ny)
            part = jnp.dot(t2[...], value, precision=HIGH, preferred_element_type=jnp.float32)
            for q in range(2):
                p_flat[pl.ds(2 * c + q, ngx, stride=8), :] = part[q * ngx : (q + 1) * ngx]
        for q in (6, 7):
            p_flat[pl.ds(q, ngx, stride=8), :] = jnp.zeros((ngx, ny), jnp.float32)

        def send(d, carry):
            pltpu.make_async_remote_copy(
                src_ref=p_buf.at[s, xpeer(d)],
                dst_ref=s_buf.at[s, d - 1],
                send_sem=gx_send.at[s],
                recv_sem=gx_recv.at[s],
                device_id=(xpeer(d), gz),
                device_id_type=MESH,
            ).start()
            return carry

        each_far(ngx, send)
        s_buf[s, ngx - 1] = p_buf[s, gx]

    def finish_gx(s):
        wait_bytes(s_buf.at[s, 0 : ngx - 1], gx_recv.at[s])
        coefs = jnp.sum(s_buf[s], axis=0)
        energy = jnp.sum(coefs * coefs) * (1.0 / ny)
        own = KZ // ngz
        wave = (gx // own) * KZ + gz * own + lax.rem(gx, own)
        energy = jnp.full((1, ny), energy, jnp.float32)
        goal = jnp.full((1, ny), target[wave], jnp.float32)
        ratio = (energy - goal) / (energy + goal)
        term[pl.ds(s, 1), :] = ratio * ratio

    def local_reward(s):
        offset = interior(s + 1, 0) - mean[...].reshape(1, 1, ny)
        square = offset * offset
        wide = jnp.concatenate([square[x] for x in range(nx)], axis=1)
        pick = (
            lax.broadcasted_iota(jnp.int32, (nx, nx * ny), 1) // ny
            == lax.broadcasted_iota(jnp.int32, (nx, nx * ny), 0)
        ).astype(jnp.float32)
        total = lax.dot_general(
            pick,
            wide,
            (((1,), (1,)), ((), ())),
            precision=HIGH,
            preferred_element_type=jnp.float32,
        )
        loc[s] = total * (-1.0 / ny)

    term[...] = jnp.zeros_like(term)
    load_vel.wait()
    pl.semaphore_wait(barrier, ngx + ngz + 2)
    start_halo(0, 4)
    for load in (load_t1, load_t2, load_mean, load_past, load_boot):
        load.wait()

    def viscosity(s, head, end):
        def each(i, carry):
            part = field[0, 3, i, head:end, :]
            nu[s, i, head:end, :] = BASE_VISCOSITY + part[:, s : s + 1] * wall
            return carry

        lax.fori_loop(0, nx + 2 * HALO + 1, each, 0)

    wait_x(0, 4)
    viscosity(0, 0, nz)

    def body(s, carry):
        stages(s, True)

        @pl.when(s == 0)
        def _():
            wait_z(0, 4)
            viscosity(0, nz, span)

        @pl.when(s >= 1)
        def _():
            wait_z(s, 3)

        stages(s, False)
        settle(s)

        @pl.when(s < steps - 1)
        def _():
            start_halo(s + 1, 3)

        start_gz(s)
        local_reward(s)
        for later in range(1, steps):
            pl.when(s == later - 1)(functools.partial(viscosity, later, 0, span))

        @pl.when(s >= 1)
        def _():
            start_gx(s - 1)

        @pl.when(s >= 2)
        def _():
            finish_gx(s - 2)

        @pl.when(s < steps - 1)
        def _():
            wait_x(s + 1, 3)

        return carry

    lax.fori_loop(0, steps, body, 0)

    store_vel = pltpu.make_async_copy(
        field.at[steps, 0:3, pl.ds(HALO + 1, nx), 0:nz, :], out_vel, local_sem.at[0]
    )
    store_vel.start()
    start_gx(steps - 1)
    finish_gx(steps - 2)

    plain = [None] * (past_steps + steps)
    running = boot[...]
    for t in range(past_steps + steps - 1, -1, -1):
        reward = past[t] if t < past_steps else loc[t - past_steps]
        running = reward + DISCOUNT * running
        plain[t] = running

    finish_gx(steps - 1)

    def send_x(d, carry):
        pltpu.make_async_remote_copy(
            src_ref=term,
            dst_ref=a_buf.at[d - 1],
            send_sem=ar_send.at[0],
            recv_sem=ar_recv.at[0],
            device_id=(xpeer(d), gz),
            device_id_type=MESH,
        ).start()
        return carry

    each_far(ngx, send_x)
    wait_bytes(a_buf, ar_recv.at[0])
    b_tile[...] = term[...] + jnp.sum(a_buf[...], axis=0)

    def send_z(d, carry):
        pltpu.make_async_remote_copy(
            src_ref=b_tile,
            dst_ref=b_buf.at[d - 1],
            send_sem=ar_send.at[1],
            recv_sem=ar_recv.at[1],
            device_id=(gx, zpeer(d)),
            device_id_type=MESH,
        ).start()
        return carry

    each_far(ngz, send_z)
    wait_bytes(b_buf, ar_recv.at[1])
    spectrum = (b_tile[...] + jnp.sum(b_buf[...], axis=0)) * (-1.0 / KX)

    extra = None
    for t in range(past_steps + steps - 1, -1, -1):
        if extra is not None:
            extra = extra * DISCOUNT
        if t >= past_steps:
            new = spectrum[t - past_steps : t - past_steps + 1, 0:nz]
            extra = new if extra is None else extra + new
        out_ret[t] = plain[t] + extra
    store_ret = pltpu.make_async_copy(out_ret, out_hbm, local_sem.at[1])
    store_ret.start()

    def drain(s, carry):
        wait_bytes(r_buf.at[s, 0 : ngz - 1], gz_send.at[s])
        wait_bytes(s_buf.at[s, 0 : ngx - 1], gx_send.at[s])
        return carry

    lax.fori_loop(0, steps, drain, 0)
    wait_sent(0, 4)
    for s in range(1, steps):
        wait_sent(s, 3)
    wait_bytes(a_buf, ar_send.at[0])
    wait_bytes(b_buf, ar_send.at[1])
    store_vel.wait()
    store_ret.wait()


def place(vel, ret, out_vel, out_ret):
    out_vel[...] = vel[...]
    out_ret[...] = ret[...]


def on_device(
    ngx, ngz, velocity, eddy_viscosity, target_spectrum, mean_profile, past_rewards, bootstrap_values
):
    nx, nz, ny = velocity.shape[1:]
    steps = eddy_viscosity.shape[0]
    horizon = past_rewards.shape[0] + steps
    t1 = z_table(ngz, nx, nz, nx * ngx, nz * ngz)
    t2 = x_table(ngx, ngz, nx, nx * ngx)
    span = nz + 2 * HALO
    lines = nx + 2 * HALO + 3
    f32 = jnp.float32
    hbm = pl.BlockSpec(memory_space=pltpu.HBM)
    free = pl.BlockSpec(memory_space=pl.ANY)
    smem = pl.BlockSpec(memory_space=pltpu.SMEM)
    dma = pltpu.SemaphoreType.DMA
    found = pl.pallas_call(
        functools.partial(kernel, ngx, ngz),
        out_shape=(
            jax.ShapeDtypeStruct(velocity.shape, f32),
            jax.ShapeDtypeStruct((horizon, nx, nz), f32),
        ),
        in_specs=[hbm, hbm, smem, hbm, hbm, hbm, hbm, hbm],
        out_specs=(free, free),
        scratch_shapes=[
            pltpu.VMEM(eddy_viscosity.shape, f32),
            pltpu.VMEM((1, ny), f32),
            pltpu.VMEM(past_rewards.shape, f32),
            pltpu.VMEM(bootstrap_values.shape, f32),
            pltpu.VMEM((horizon, nx, nz), f32),
            pltpu.VMEM((3, lines * span, ny), f32),
            pltpu.VMEM((steps + 1, 4, lines, span, ny), f32),
            pltpu.VMEM((3, lines * span, ny), f32),
            pltpu.VMEM((3, lines * span, ny), f32),
            pltpu.VMEM((3, lines * span, ny), f32),
            pltpu.VMEM((steps, lines, span, ny), f32),
            pltpu.VMEM((steps, 2, 4, nx, HALO, ny), f32),
            pltpu.VMEM((steps, 2, 4, nx, HALO, ny), f32),
            pltpu.VMEM((steps, 4, 4, 8, ny), f32),
            pltpu.VMEM((steps, 4, 4, 8, ny), f32),
            pltpu.VMEM(t1.shape[1:], f32),
            pltpu.VMEM(t2.shape[1:], f32),
            pltpu.VMEM((steps, ngz, 3, t1.shape[1] // ngz, ny), f32),
            pltpu.VMEM((steps, ngz, 3, t1.shape[1] // ngz, ny), f32),
            pltpu.VMEM((steps, ngx, 8, ny), f32),
            pltpu.VMEM((steps, ngx, 8, ny), f32),
            pltpu.VMEM((steps, nx, nz), f32),
            pltpu.VMEM((8, ny), f32),
            pltpu.VMEM((ngx - 1, 8, ny), f32),
            pltpu.VMEM((8, ny), f32),
            pltpu.VMEM((ngz - 1, 8, ny), f32),
            dma((7,)),
            dma((steps, 8)),
            dma((steps, 8)),
            dma((steps,)),
            dma((steps,)),
            dma((steps,)),
            dma((steps,)),
            dma((2,)),
            dma((2,)),
        ],
        compiler_params=pltpu.CompilerParams(
            collective_id=0, has_side_effects=True, vmem_limit_bytes=62 * 1024 * 1024
        ),
        name="rollout",
    )(
        velocity,
        eddy_viscosity,
        target_spectrum,
        mean_profile.reshape(1, ny),
        past_rewards,
        bootstrap_values,
        jnp.asarray(t1),
        jnp.asarray(t2),
    )

    return pl.pallas_call(
        place,
        out_shape=tuple(jax.ShapeDtypeStruct(part.shape, f32) for part in found),
        in_specs=[pl.BlockSpec(memory_space=pltpu.VMEM)] * 2,
        out_specs=(pl.BlockSpec(memory_space=pltpu.VMEM),) * 2,
        name="place",
    )(*found)


def solution(mesh):
    placed = (
        P(None, "gx", "gz", None),
        P(None, "gx", "gz"),
        P(),
        P(),
        P(None, "gx", "gz"),
        P("gx", "gz"),
    )
    return jax.shard_map(
        functools.partial(on_device, mesh.shape["gx"], mesh.shape["gz"]),
        mesh=mesh,
        in_specs=placed,
        out_specs=(P(None, "gx", "gz", None), P(None, "gx", "gz")),
        check_vma=False,
    )
```

```python
import functools
import math

import numpy as np

import jax
import jax.numpy as jnp
from jax import lax
from jax.experimental import pallas as pl
from jax.experimental.pallas import tpu as pltpu
from jax.sharding import PartitionSpec as P

KX = 16
KZ = 16
STEP = 0.05
BASE_VISCOSITY = 0.02
DRIVE = 0.5
DISCOUNT = 0.97
HALO = 4
MESH = pl.DeviceIdType.MESH
HIGH = lax.Precision.HIGHEST


def z_table(peers, cells_x, cells_z, total_x, total_z):
    own = KZ // peers
    factor = 1.0 / math.sqrt(total_x * total_z)
    spots = np.arange(peers)[:, None] * cells_z + np.arange(cells_z)[None, :]
    turns = (np.arange(KZ)[None, :, None] * spots[:, None, :]) % total_z
    angle = turns * (2.0 * math.pi / total_z)
    waves = np.stack([np.cos(angle), -np.sin(angle)], axis=2) * factor
    eye = np.eye(cells_x)
    table = np.einsum("gkrz,ab->gkraBz".replace("B", "b"), waves, eye)
    rows = peers * own * 2 * cells_x
    return table.reshape(peers, rows, cells_x * cells_z).astype(np.float32)


def x_table(devices, peers, cells_x, total_x):
    own = KZ // peers
    spots = np.arange(devices)[:, None] * cells_x + np.arange(cells_x)[None, :]
    turns = (np.arange(KX)[None, :, None] * spots[:, None, :]) % total_x
    angle = turns * (2.0 * math.pi / total_x)
    c, s = np.cos(angle), np.sin(angle)
    spin = np.stack([np.stack([c, s], 2), np.stack([-s, c], 2)], 1)
    eye = np.eye(own)
    table = np.einsum("gqkrx,ab->gqkabrx", spin, eye)
    table = table.reshape(devices, 2 * KX * own, 1, own * 2 * cells_x)
    table = np.broadcast_to(table, (devices, 2 * KX * own, peers, own * 2 * cells_x))
    return table.reshape(devices, 2 * KX * own, peers * own * 2 * cells_x).astype(np.float32)


def kernel(
    ngx,
    ngz,
    vel,
    eddy_hbm,
    target,
    mean_hbm,
    past_hbm,
    boot_hbm,
    t1_hbm,
    t2_hbm,
    out_vel,
    out_hbm,
    eddy,
    mean,
    past,
    boot,
    out_ret,
    fresh,
    field,
    w2,
    w3,
    w4,
    nu,
    pack,
    zc,
    corner_out,
    corner_in,
    t1,
    t2,
    q_buf,
    r_buf,
    p_buf,
    s_buf,
    loc,
    term,
    a_buf,
    b_tile,
    b_buf,
    local_sem,
    halo_send,
    halo_recv,
    gz_send,
    gz_recv,
    gx_send,
    gx_recv,
    ar_send,
    ar_recv,
):
    gx = lax.axis_index("gx")
    gz = lax.axis_index("gz")
    steps = eddy.shape[0]
    nx = vel.shape[1]
    nz = vel.shape[2]
    ny = vel.shape[3]
    span = nz + 2 * HALO
    rows = (nx + 2 * HALO + 3) * span
    past_steps = past.shape[0]

    def each_far(count, send):
        for step in range(count - 1):
            away = (step + 1) // 2
            send(count // 2 + (away if step % 2 else -away), 0)

    def xpeer(d):
        return lax.rem(gx + d + ngx, ngx)

    def zpeer(d):
        return lax.rem(gz + d + ngz, ngz)

    barrier = pltpu.get_barrier_semaphore()

    def greet_x(d, carry):
        pl.semaphore_signal(barrier, inc=1, device_id=(xpeer(d), gz), device_id_type=MESH)
        return carry

    def greet_z(d, carry):
        pl.semaphore_signal(barrier, inc=1, device_id=(gx, zpeer(d)), device_id_type=MESH)
        return carry

    each_far(ngx, greet_x)
    each_far(ngz, greet_z)
    for dx in (-1, 1):
        for dz in (-1, 1):
            pl.semaphore_signal(
                barrier, inc=1, device_id=(xpeer(dx), zpeer(dz)), device_id_type=MESH
            )

    load_vel = pltpu.make_async_copy(
        vel, field.at[0, 0:3, pl.ds(HALO + 1, nx), 0:nz, :], local_sem.at[0]
    )
    load_t1 = pltpu.make_async_copy(t1_hbm.at[gz], t1, local_sem.at[1])
    load_t2 = pltpu.make_async_copy(t2_hbm.at[gx], t2, local_sem.at[2])
    load_eddy = pltpu.make_async_copy(eddy_hbm, eddy, local_sem.at[3])
    load_mean = pltpu.make_async_copy(mean_hbm, mean, local_sem.at[4])
    load_past = pltpu.make_async_copy(past_hbm, past, local_sem.at[5])
    load_boot = pltpu.make_async_copy(boot_hbm, boot, local_sem.at[6])
    load_eddy.start()
    load_vel.start()
    for load in (load_t1, load_t2, load_mean, load_past, load_boot):
        load.start()

    load_eddy.wait()
    eye = (
        lax.broadcasted_iota(jnp.int32, (steps, ny), 0)
        == lax.broadcasted_iota(jnp.int32, (steps, ny), 1)
    ).astype(jnp.float32)
    for x in range(nx):
        field[0, 3, HALO + 1 + x, 0:nz, :] = lax.dot_general(
            eddy[:, x, :],
            eye,
            (((0,), (0,)), ((), ())),
            precision=HIGH,
            preferred_element_type=jnp.float32,
        )

    first = HALO + 1
    corners = [(dx, dz) for dx in (1, -1) for dz in (1, -1)]

    def halo_copies(s, comps):
        copies = []
        for index, (dx, dz) in enumerate(corners):
            copies.append((corner_out.at[s, index, 0:comps], corner_in.at[s, index, 0:comps], dx, dz))
        for side, dz in ((0, 1), (1, -1)):
            copies.append((pack.at[s, side, 0:comps], zc.at[s, side, 0:comps], 0, dz))
        for dx, src, dst in ((1, first + nx - HALO, 1), (-1, first, first + nx)):
            copies.append(
                (
                    field.at[s, 0:comps, pl.ds(src, HALO), 0:nz, :],
                    field.at[s, 0:comps, pl.ds(dst, HALO), 0:nz, :],
                    dx,
                    0,
                )
            )
        return [
            pltpu.make_async_remote_copy(
                src_ref=src,
                dst_ref=dst,
                send_sem=halo_send.at[s, index],
                recv_sem=halo_recv.at[s, index],
                device_id=(xpeer(dx), zpeer(dz)),
                device_id_type=MESH,
            )
            for index, (src, dst, dx, dz) in enumerate(copies)
        ]

    diamond = []
    taken = 0
    for away in range(1, HALO):
        diamond.append((away, taken, HALO - away))
        taken += HALO - away

    def start_edges(s, comps, source):
        for index, (dx, dz) in enumerate(corners):
            for c in range(comps):
                for away, at, count in diamond:
                    line = first + nx - away if dx == 1 else first + away - 1
                    head = nz - count if dz == 1 else 0
                    corner_out[s, index, c, at : at + count, :] = source[
                        c, line, head : head + count, :
                    ]
        for c in range(comps):
            pack[s, 0, c] = source[c, pl.ds(first, nx), nz - HALO : nz, :]
            pack[s, 1, c] = source[c, pl.ds(first, nx), 0:HALO, :]
        for copy in halo_copies(s, comps)[:6]:
            copy.start()

    def start_lines(s, comps):
        for copy in halo_copies(s, comps)[6:]:
            copy.start()

    def wait_x(s, comps):
        for copy in halo_copies(s, comps)[6:]:
            copy.wait_recv()

    def wait_z(s, comps):
        for copy in halo_copies(s, comps)[:6]:
            copy.wait_recv()
        for c in range(comps):
            field[s, c, pl.ds(first - 1, nx), nz + HALO : span, :] = zc[s, 0, c]
            field[s, c, pl.ds(first, nx), nz : nz + HALO, :] = zc[s, 1, c]
        for index, (dx, dz) in enumerate(corners):
            for c in range(comps):
                for away, at, count in diamond:
                    line = first - away if dx == 1 else first + nx - 1 + away
                    if dz == 1:
                        line, head = line - 1, span - count
                    else:
                        head = nz
                    field[s, c, line, head : head + count, :] = corner_in[
                        s, index, c, at : at + count, :
                    ]

    def wait_sent(s, comps):
        for copy in halo_copies(s, comps):
            copy.wait_send()

    lane = lax.broadcasted_iota(jnp.int32, (8, ny), 1)
    mask_plus = (lane < ny - 1).astype(jnp.float32)
    mask_minus = (lane > 0).astype(jnp.float32)
    rows_y = lane[0:1].astype(jnp.float32) + 0.5
    wall = jnp.minimum(rows_y, ny - rows_y) / (ny / 2.0)

    def here(r):
        return pl.ds(pl.multiple_of(r, 8), 8)

    def advance(src, nu_s, r, scale, base):
        mid = [src[c, here(r), :] for c in range(3)]
        visc = nu_s[here(r), :] * scale
        half = 0.5 * scale
        hu, hw, hv = mid[0] * half, mid[1] * half, mid[2] * half
        x_plus, x_minus = visc - hu, visc + hu
        z_plus, z_minus = visc - hw, visc + hw
        y_plus, y_minus = (visc - hv) * mask_plus, (visc + hv) * mask_minus
        center = visc * -6.0
        if base is None:
            center = center + 1.0
        out = []
        for c in range(3):
            around = src.at[c, pl.ds(pl.multiple_of(r - 8, 8), 24), :]
            value = center * mid[c]
            if base is not None:
                value += base(c, mid[c])
            if c == 0:
                value += DRIVE * scale
            value += x_plus * src[c, here(r + span), :]
            value += x_minus * src[c, here(r - span), :]
            value += z_plus * around[9:17, :]
            value += z_minus * around[7:15, :]
            value += y_plus * pltpu.roll(mid[c], ny - 1, 1)
            value += y_minus * pltpu.roll(mid[c], 1, 1)
            out.append(value)
        return out

    def stages(s, inner):
        v0 = field.at[s].reshape(4, rows, ny)
        nu_s = nu.at[s].reshape(rows, ny)
        total = nx + 2 * HALO

        def start_value(r):
            return lambda c, mid: v0[c, here(r), :]

        def last_value(r):
            return lambda c, mid: (
                (w2[c, here(r), :] + mid - v0[c, here(r), :]) + 2.0 * w3[c, here(r), :]
            ) * (1.0 / 3.0)

        plan = (
            (v0, w2, 0.5 * STEP, lambda r: None),
            (w2, w3, 0.5 * STEP, start_value),
            (w3, w4, STEP, start_value),
            (w4, fresh, STEP / 6.0, last_value),
        )
        for k, (src, dst, scale, base) in enumerate(plan, 1):
            final = k == len(plan)
            if inner:
                tiles = range(8, nz - 8, 8) if final else range(0, nz, 8)
            else:
                tiles = (0, nz - 8) if final else (-8, 0, nz - 8)

            def one(r, src=src, dst=dst, scale=scale, base=base):
                out = advance(src, nu_s, r, scale, base(r))
                for c in range(3):
                    dst[c, here(r), :] = out[c]

            def line(i, carry, k=k, one=one, tiles=tiles):
                for t in tiles:
                    one((k + 1 + i) * span + t)
                return carry

            lax.fori_loop(0, total - 2 * k, line, 0, unroll=True)
            if not inner and not final:
                one((total + 1 - k) * span - 8)

    def settle(s):
        for c in range(3):
            for x in range(nx):
                field[s + 1, c, first + x, 0:nz, :] = fresh[c, pl.ds((first + x) * span, nz), :]

    def interior(s, c):
        return field[s, c, pl.ds(HALO + 1, nx), 0:nz, :]

    def start_gz(s):
        cells = nx * nz
        for c in range(3):
            value = interior(s + 1, c).reshape(cells, ny)
            part = jnp.dot(t1[...], value, precision=HIGH, preferred_element_type=jnp.float32)
            q_buf[s, :, c] = part.reshape(ngz, part.shape[0] // ngz, ny)

        def send(d, carry):
            pltpu.make_async_remote_copy(
                src_ref=q_buf.at[s, zpeer(d)],
                dst_ref=r_buf.at[s, d - 1],
                send_sem=gz_send.at[s],
                recv_sem=gz_recv.at[s],
                device_id=(gx, zpeer(d)),
                device_id_type=MESH,
            ).start()
            return carry

        each_far(ngz, send)
        r_buf[s, ngz - 1] = q_buf[s, gz]

    def wait_bytes(ref, sem):
        pltpu.make_async_copy(ref, ref, sem).wait()

    def start_gx(s):
        wait_bytes(r_buf.at[s, 0 : ngz - 1], gz_recv.at[s])
        for c in range(3):
            value = r_buf[s, :, c].reshape(t2.shape[1], ny)
            part = jnp.dot(t2[...], value, precision=HIGH, preferred_element_type=jnp.float32)
            for q in range(2):
                p_buf[s, :, c, q, :] = part[q * ngx : (q + 1) * ngx]

        def send(d, carry):
            pltpu.make_async_remote_copy(
                src_ref=p_buf.at[s, xpeer(d)],
                dst_ref=s_buf.at[s, d - 1],
                send_sem=gx_send.at[s],
                recv_sem=gx_recv.at[s],
                device_id=(xpeer(d), gz),
                device_id_type=MESH,
            ).start()
            return carry

        each_far(ngx, send)
        s_buf[s, ngx - 1] = p_buf[s, gx]

    def finish_gx(s):
        wait_bytes(s_buf.at[s, 0 : ngx - 1], gx_recv.at[s])
        coefs = jnp.sum(s_buf[s], axis=0)
        energy = jnp.sum(jnp.sum(coefs * coefs, axis=0), axis=(0, 1), keepdims=True) * (1.0 / ny)
        own = KZ // ngz
        wave = (gx // own) * KZ + gz * own + lax.rem(gx, own)
        energy = jnp.broadcast_to(energy, (1, ny))
        goal = jnp.full((1, ny), target[wave], jnp.float32)
        ratio = (energy - goal) / (energy + goal)
        term[...] += jnp.where(lane[0:1] == s, ratio * ratio, 0.0)

    def local_reward(s):
        offset = interior(s + 1, 0) - mean[...].reshape(1, 1, ny)
        square = offset * offset
        wide = jnp.concatenate([square[x] for x in range(nx)], axis=1)
        pick = (
            lax.broadcasted_iota(jnp.int32, (nx, nx * ny), 1) // ny
            == lax.broadcasted_iota(jnp.int32, (nx, nx * ny), 0)
        ).astype(jnp.float32)
        total = lax.dot_general(
            pick,
            wide,
            (((1,), (1,)), ((), ())),
            precision=HIGH,
            preferred_element_type=jnp.float32,
        )
        loc[s] = total * (-1.0 / ny)

    term[...] = jnp.zeros_like(term)
    load_vel.wait()
    pl.semaphore_wait(barrier, ngx + ngz + 2)
    start_edges(0, 4, field.at[0])
    start_lines(0, 4)
    for load in (load_t1, load_t2, load_mean, load_past, load_boot):
        load.wait()

    def viscosity(s, head, end):
        def each(i, carry):
            part = field[0, 3, i, head:end, :]
            nu[s, i, head:end, :] = BASE_VISCOSITY + part[:, s : s + 1] * wall
            return carry

        lax.fori_loop(0, nx + 2 * HALO + 1, each, 0)

    wait_x(0, 4)
    viscosity(0, 0, nz)

    def body(s, carry):
        stages(s, True)

        @pl.when(s == 0)
        def _():
            wait_z(0, 4)
            viscosity(0, nz, span)

        @pl.when(s >= 1)
        def _():
            wait_z(s, 3)

        stages(s, False)

        @pl.when(s < steps - 1)
        def _():
            start_edges(s + 1, 3, fresh.reshape(3, rows // span, span, ny))

        settle(s)

        @pl.when(s < steps - 1)
        def _():
            start_lines(s + 1, 3)

        start_gz(s)
        local_reward(s)
        for later in range(1, steps):
            pl.when(s == later - 1)(functools.partial(viscosity, later, 0, span))

        @pl.when(s >= 1)
        def _():
            start_gx(s - 1)

        @pl.when(s >= 2)
        def _():
            finish_gx(s - 2)

        @pl.when(s < steps - 1)
        def _():
            wait_x(s + 1, 3)

        return carry

    lax.fori_loop(0, steps, body, 0)

    store_vel = pltpu.make_async_copy(
        field.at[steps, 0:3, pl.ds(HALO + 1, nx), 0:nz, :], out_vel, local_sem.at[0]
    )
    store_vel.start()
    start_gx(steps - 1)
    finish_gx(steps - 2)

    plain = [None] * (past_steps + steps)
    running = boot[...]
    for t in range(past_steps + steps - 1, -1, -1):
        reward = past[t] if t < past_steps else loc[t - past_steps]
        running = reward + DISCOUNT * running
        plain[t] = running

    finish_gx(steps - 1)

    def send_x(d, carry):
        pltpu.make_async_remote_copy(
            src_ref=term,
            dst_ref=a_buf.at[d - 1],
            send_sem=ar_send.at[0],
            recv_sem=ar_recv.at[0],
            device_id=(xpeer(d), gz),
            device_id_type=MESH,
        ).start()
        return carry

    each_far(ngx, send_x)
    wait_bytes(a_buf, ar_recv.at[0])
    b_tile[...] = term[...] + jnp.sum(a_buf[...], axis=0)

    def send_z(d, carry):
        pltpu.make_async_remote_copy(
            src_ref=b_tile,
            dst_ref=b_buf.at[d - 1],
            send_sem=ar_send.at[1],
            recv_sem=ar_recv.at[1],
            device_id=(gx, zpeer(d)),
            device_id_type=MESH,
        ).start()
        return carry

    each_far(ngz, send_z)
    wait_bytes(b_buf, ar_recv.at[1])
    spectrum = (b_tile[...] + jnp.sum(b_buf[...], axis=0)) * (-1.0 / KX)

    extra = None
    for t in range(past_steps + steps - 1, -1, -1):
        if extra is not None:
            extra = extra * DISCOUNT
        if t >= past_steps:
            new = spectrum[:, t - past_steps : t - past_steps + 1]
            extra = new if extra is None else extra + new
        out_ret[t] = plain[t] + extra
    store_ret = pltpu.make_async_copy(out_ret, out_hbm, local_sem.at[1])
    store_ret.start()

    def drain(s, carry):
        wait_bytes(r_buf.at[s, 0 : ngz - 1], gz_send.at[s])
        wait_bytes(s_buf.at[s, 0 : ngx - 1], gx_send.at[s])
        return carry

    lax.fori_loop(0, steps, drain, 0)
    wait_sent(0, 4)
    for s in range(1, steps):
        wait_sent(s, 3)
    wait_bytes(a_buf, ar_send.at[0])
    wait_bytes(b_buf, ar_send.at[1])
    store_vel.wait()
    store_ret.wait()


def place(vel, ret, out_vel, out_ret):
    out_vel[...] = vel[...]
    out_ret[...] = ret[...]


def on_device(
    ngx, ngz, velocity, eddy_viscosity, target_spectrum, mean_profile, past_rewards, bootstrap_values
):
    nx, nz, ny = velocity.shape[1:]
    steps = eddy_viscosity.shape[0]
    horizon = past_rewards.shape[0] + steps
    t1 = z_table(ngz, nx, nz, nx * ngx, nz * ngz)
    t2 = x_table(ngx, ngz, nx, nx * ngx)
    span = nz + 2 * HALO
    lines = nx + 2 * HALO + 3
    f32 = jnp.float32
    hbm = pl.BlockSpec(memory_space=pltpu.HBM)
    free = pl.BlockSpec(memory_space=pl.ANY)
    smem = pl.BlockSpec(memory_space=pltpu.SMEM)
    dma = pltpu.SemaphoreType.DMA
    found = pl.pallas_call(
        functools.partial(kernel, ngx, ngz),
        out_shape=(
            jax.ShapeDtypeStruct(velocity.shape, f32),
            jax.ShapeDtypeStruct((horizon, nx, nz), f32),
        ),
        in_specs=[hbm, hbm, smem, hbm, hbm, hbm, hbm, hbm],
        out_specs=(free, free),
        scratch_shapes=[
            pltpu.VMEM(eddy_viscosity.shape, f32),
            pltpu.VMEM((1, ny), f32),
            pltpu.VMEM(past_rewards.shape, f32),
            pltpu.VMEM(bootstrap_values.shape, f32),
            pltpu.VMEM((horizon, nx, nz), f32),
            pltpu.VMEM((3, lines * span, ny), f32),
            pltpu.VMEM((steps + 1, 4, lines, span, ny), f32),
            pltpu.VMEM((3, lines * span, ny), f32),
            pltpu.VMEM((3, lines * span, ny), f32),
            pltpu.VMEM((3, lines * span, ny), f32),
            pltpu.VMEM((steps, lines, span, ny), f32),
            pltpu.VMEM((steps, 2, 4, nx, HALO, ny), f32),
            pltpu.VMEM((steps, 2, 4, nx, HALO, ny), f32),
            pltpu.VMEM((steps, 4, 4, 8, ny), f32),
            pltpu.VMEM((steps, 4, 4, 8, ny), f32),
            pltpu.VMEM(t1.shape[1:], f32),
            pltpu.VMEM(t2.shape[1:], f32),
            pltpu.VMEM((steps, ngz, 3, t1.shape[1] // ngz, ny), f32),
            pltpu.VMEM((steps, ngz, 3, t1.shape[1] // ngz, ny), f32),
            pltpu.VMEM((steps, ngx, 3, 2, ny), f32),
            pltpu.VMEM((steps, ngx, 3, 2, ny), f32),
            pltpu.VMEM((steps, nx, nz), f32),
            pltpu.VMEM((1, ny), f32),
            pltpu.VMEM((ngx - 1, 1, ny), f32),
            pltpu.VMEM((1, ny), f32),
            pltpu.VMEM((ngz - 1, 1, ny), f32),
            dma((7,)),
            dma((steps, 8)),
            dma((steps, 8)),
            dma((steps,)),
            dma((steps,)),
            dma((steps,)),
            dma((steps,)),
            dma((2,)),
            dma((2,)),
        ],
        compiler_params=pltpu.CompilerParams(
            collective_id=0, has_side_effects=True, vmem_limit_bytes=62 * 1024 * 1024
        ),
        name="rollout",
    )(
        velocity,
        eddy_viscosity,
        target_spectrum,
        mean_profile.reshape(1, ny),
        past_rewards,
        bootstrap_values,
        jnp.asarray(t1),
        jnp.asarray(t2),
    )

    return pl.pallas_call(
        place,
        out_shape=tuple(jax.ShapeDtypeStruct(part.shape, f32) for part in found),
        in_specs=[pl.BlockSpec(memory_space=pltpu.VMEM)] * 2,
        out_specs=(pl.BlockSpec(memory_space=pltpu.VMEM),) * 2,
        name="place",
    )(*found)


def solution(mesh):
    placed = (
        P(None, "gx", "gz", None),
        P(None, "gx", "gz"),
        P(),
        P(),
        P(None, "gx", "gz"),
        P("gx", "gz"),
    )
    return jax.shard_map(
        functools.partial(on_device, mesh.shape["gx"], mesh.shape["gz"]),
        mesh=mesh,
        in_specs=placed,
        out_specs=(P(None, "gx", "gz", None), P(None, "gx", "gz")),
        check_vma=False,
    )
```

```python
import functools
import math

import numpy as np

import jax
import jax.numpy as jnp
from jax import lax
from jax.experimental import pallas as pl
from jax.experimental.pallas import tpu as pltpu
from jax.sharding import PartitionSpec as P

KX = 16
KZ = 16
STEP = 0.05
BASE_VISCOSITY = 0.02
DRIVE = 0.5
DISCOUNT = 0.97
HALO = 4
MESH = pl.DeviceIdType.MESH
HIGH = lax.Precision.HIGHEST


def z_table(peers, cells_x, cells_z, total_x, total_z):
    own = KZ // peers
    factor = 1.0 / math.sqrt(total_x * total_z)
    spots = np.arange(peers)[:, None] * cells_z + np.arange(cells_z)[None, :]
    turns = (np.arange(KZ)[None, :, None] * spots[:, None, :]) % total_z
    angle = turns * (2.0 * math.pi / total_z)
    waves = np.stack([np.cos(angle), -np.sin(angle)], axis=2) * factor
    eye = np.eye(cells_x)
    table = np.einsum("gkrz,ab->gkraBz".replace("B", "b"), waves, eye)
    rows = peers * own * 2 * cells_x
    return table.reshape(peers, rows, cells_x * cells_z).astype(np.float32)


def x_table(devices, peers, cells_x, total_x):
    own = KZ // peers
    spots = np.arange(devices)[:, None] * cells_x + np.arange(cells_x)[None, :]
    turns = (np.arange(KX)[None, :, None] * spots[:, None, :]) % total_x
    angle = turns * (2.0 * math.pi / total_x)
    c, s = np.cos(angle), np.sin(angle)
    spin = np.stack([np.stack([c, s], 2), np.stack([-s, c], 2)], 1)
    eye = np.eye(own)
    table = np.einsum("gqkrx,ab->gqkabrx", spin, eye)
    table = table.reshape(devices, 2 * KX * own, 1, own * 2 * cells_x)
    table = np.broadcast_to(table, (devices, 2 * KX * own, peers, own * 2 * cells_x))
    return table.reshape(devices, 2 * KX * own, peers * own * 2 * cells_x).astype(np.float32)


def kernel(
    ngx,
    ngz,
    vel,
    eddy_hbm,
    target,
    mean_hbm,
    past_hbm,
    boot_hbm,
    t1_hbm,
    t2_hbm,
    out_vel,
    out_hbm,
    eddy,
    mean,
    past,
    boot,
    out_ret,
    fresh,
    field,
    w2,
    w3,
    w4,
    nu,
    pack,
    zc,
    corner_out,
    corner_in,
    t1,
    t2,
    q_buf,
    r_buf,
    p_buf,
    s_buf,
    loc,
    term,
    a_buf,
    b_tile,
    b_buf,
    local_sem,
    halo_send,
    halo_recv,
    gz_send,
    gz_recv,
    gx_send,
    gx_recv,
    ar_send,
    ar_recv,
):
    gx = lax.axis_index("gx")
    gz = lax.axis_index("gz")
    steps = eddy.shape[0]
    nx = vel.shape[1]
    nz = vel.shape[2]
    ny = vel.shape[3]
    span = nz + 2 * HALO
    rows = (nx + 2 * HALO + 3) * span
    past_steps = past.shape[0]

    def each_far(count, send):
        for step in range(count - 1):
            away = (step + 1) // 2
            send(count // 2 + (away if step % 2 else -away), 0)

    def xpeer(d):
        return lax.rem(gx + d + ngx, ngx)

    def zpeer(d):
        return lax.rem(gz + d + ngz, ngz)

    barrier = pltpu.get_barrier_semaphore()

    def greet_x(d, carry):
        pl.semaphore_signal(barrier, inc=1, device_id=(xpeer(d), gz), device_id_type=MESH)
        return carry

    def greet_z(d, carry):
        pl.semaphore_signal(barrier, inc=1, device_id=(gx, zpeer(d)), device_id_type=MESH)
        return carry

    each_far(ngx, greet_x)
    each_far(ngz, greet_z)
    for dx in (-1, 1):
        for dz in (-1, 1):
            pl.semaphore_signal(
                barrier, inc=1, device_id=(xpeer(dx), zpeer(dz)), device_id_type=MESH
            )

    load_vel = pltpu.make_async_copy(
        vel, field.at[0, 0:3, pl.ds(HALO + 1, nx), 0:nz, :], local_sem.at[0]
    )
    load_t1 = pltpu.make_async_copy(t1_hbm.at[gz], t1, local_sem.at[1])
    load_t2 = pltpu.make_async_copy(t2_hbm.at[gx], t2, local_sem.at[2])
    load_eddy = pltpu.make_async_copy(eddy_hbm, eddy, local_sem.at[3])
    load_mean = pltpu.make_async_copy(mean_hbm, mean, local_sem.at[4])
    load_past = pltpu.make_async_copy(past_hbm, past, local_sem.at[5])
    load_boot = pltpu.make_async_copy(boot_hbm, boot, local_sem.at[6])
    load_eddy.start()
    load_vel.start()
    for load in (load_t1, load_t2, load_mean, load_past, load_boot):
        load.start()

    load_eddy.wait()
    eye = (
        lax.broadcasted_iota(jnp.int32, (steps, ny), 0)
        == lax.broadcasted_iota(jnp.int32, (steps, ny), 1)
    ).astype(jnp.float32)
    for x in range(nx):
        field[0, 3, HALO + 1 + x, 0:nz, :] = lax.dot_general(
            eddy[:, x, :],
            eye,
            (((0,), (0,)), ((), ())),
            precision=HIGH,
            preferred_element_type=jnp.float32,
        )

    first = HALO + 1
    corners = [(dx, dz) for dx in (1, -1) for dz in (1, -1)]

    def halo_copies(s, comps):
        source = field.at[0] if comps == 4 else fresh
        copies = []
        for index, (dx, dz) in enumerate(corners):
            copies.append((corner_out.at[s, index, 0:comps], corner_in.at[s, index, 0:comps], dx, dz))
        for side, dz in ((0, 1), (1, -1)):
            copies.append((pack.at[s, side, 0:comps], zc.at[s, side, 0:comps], 0, dz))
        for dx, src, dst in ((1, first + nx - HALO, 1), (-1, first, first + nx)):
            copies.append(
                (
                    source.at[0:comps, pl.ds(src, HALO), 0:nz, :],
                    field.at[s, 0:comps, pl.ds(dst, HALO), 0:nz, :],
                    dx,
                    0,
                )
            )
        return [
            pltpu.make_async_remote_copy(
                src_ref=src,
                dst_ref=dst,
                send_sem=halo_send.at[s, index],
                recv_sem=halo_recv.at[s, index],
                device_id=(xpeer(dx), zpeer(dz)),
                device_id_type=MESH,
            )
            for index, (src, dst, dx, dz) in enumerate(copies)
        ]

    diamond = []
    taken = 0
    for away in range(1, HALO):
        diamond.append((away, taken, HALO - away))
        taken += HALO - away

    def start_edges(s, comps, source):
        for index, (dx, dz) in enumerate(corners):
            for c in range(comps):
                for away, at, count in diamond:
                    line = first + nx - away if dx == 1 else first + away - 1
                    head = nz - count if dz == 1 else 0
                    corner_out[s, index, c, at : at + count, :] = source[
                        c, line, head : head + count, :
                    ]
        for c in range(comps):
            pack[s, 0, c] = source[c, pl.ds(first, nx), nz - HALO : nz, :]
            pack[s, 1, c] = source[c, pl.ds(first, nx), 0:HALO, :]
        for copy in halo_copies(s, comps)[:6]:
            copy.start()

    def start_lines(s, comps):
        for copy in halo_copies(s, comps)[6:]:
            copy.start()

    def wait_x(s, comps):
        for copy in halo_copies(s, comps)[6:]:
            copy.wait_recv()
            copy.wait_send()

    def wait_z(s, comps):
        for copy in halo_copies(s, comps)[:6]:
            copy.wait_recv()
        for c in range(comps):
            field[s, c, pl.ds(first - 1, nx), nz + HALO : span, :] = zc[s, 0, c]
            field[s, c, pl.ds(first, nx), nz : nz + HALO, :] = zc[s, 1, c]
        for index, (dx, dz) in enumerate(corners):
            for c in range(comps):
                for away, at, count in diamond:
                    line = first - away if dx == 1 else first + nx - 1 + away
                    if dz == 1:
                        line, head = line - 1, span - count
                    else:
                        head = nz
                    field[s, c, line, head : head + count, :] = corner_in[
                        s, index, c, at : at + count, :
                    ]

    def wait_sent(s, comps):
        for copy in halo_copies(s, comps)[:6]:
            copy.wait_send()

    lane = lax.broadcasted_iota(jnp.int32, (8, ny), 1)
    mask_plus = (lane < ny - 1).astype(jnp.float32)
    mask_minus = (lane > 0).astype(jnp.float32)
    rows_y = lane[0:1].astype(jnp.float32) + 0.5
    wall = jnp.minimum(rows_y, ny - rows_y) / (ny / 2.0)

    def here(r):
        return pl.ds(pl.multiple_of(r, 8), 8)

    def advance(src, nu_s, r, scale, base):
        mid = [src[c, here(r), :] for c in range(3)]
        visc = nu_s[here(r), :] * scale
        half = 0.5 * scale
        hu, hw, hv = mid[0] * half, mid[1] * half, mid[2] * half
        x_plus, x_minus = visc - hu, visc + hu
        z_plus, z_minus = visc - hw, visc + hw
        y_plus, y_minus = (visc - hv) * mask_plus, (visc + hv) * mask_minus
        center = visc * -6.0
        if base is None:
            center = center + 1.0
        out = []
        for c in range(3):
            around = src.at[c, pl.ds(pl.multiple_of(r - 8, 8), 24), :]
            value = center * mid[c]
            if base is not None:
                value += base(c, mid[c])
            if c == 0:
                value += DRIVE * scale
            value += x_plus * src[c, here(r + span), :]
            value += x_minus * src[c, here(r - span), :]
            value += z_plus * around[9:17, :]
            value += z_minus * around[7:15, :]
            value += y_plus * pltpu.roll(mid[c], ny - 1, 1)
            value += y_minus * pltpu.roll(mid[c], 1, 1)
            out.append(value)
        return out

    def stages(s, inner):
        v0 = field.at[s].reshape(4, rows, ny)
        nu_s = nu.at[s].reshape(rows, ny)
        total = nx + 2 * HALO

        def start_value(r):
            return lambda c, mid: v0[c, here(r), :]

        def last_value(r):
            return lambda c, mid: (
                (w2[c, here(r), :] + mid - v0[c, here(r), :]) + 2.0 * w3[c, here(r), :]
            ) * (1.0 / 3.0)

        plan = (
            (v0, w2, 0.5 * STEP, lambda r: None),
            (w2, w3, 0.5 * STEP, start_value),
            (w3, w4, STEP, start_value),
            (w4, fresh.reshape(3, rows, ny), STEP / 6.0, last_value),
        )
        for k, (src, dst, scale, base) in enumerate(plan, 1):
            final = k == len(plan)
            if inner:
                tiles = range(8, nz - 8, 8) if final else range(0, nz, 8)
            else:
                tiles = (0, nz - 8) if final else (-8, 0, nz - 8)

            def one(r, src=src, dst=dst, scale=scale, base=base):
                out = advance(src, nu_s, r, scale, base(r))
                for c in range(3):
                    dst[c, here(r), :] = out[c]

            def line(i, carry, k=k, one=one, tiles=tiles):
                for t in tiles:
                    one((k + 1 + i) * span + t)
                return carry

            lax.fori_loop(0, total - 2 * k, line, 0, unroll=True)
            if not inner and not final:
                one((total + 1 - k) * span - 8)

    def settle(s):
        for c in range(3):
            for x in range(nx):
                field[s + 1, c, first + x, 0:nz, :] = fresh[c, first + x, 0:nz, :]

    def interior(s, c):
        return field[s, c, pl.ds(HALO + 1, nx), 0:nz, :]

    def start_gz(s):
        cells = nx * nz
        for c in range(3):
            value = fresh[c, pl.ds(first, nx), 0:nz, :].reshape(cells, ny)
            part = jnp.dot(t1[...], value, precision=HIGH, preferred_element_type=jnp.float32)
            q_buf[s, :, c] = part.reshape(ngz, part.shape[0] // ngz, ny)

        def send(d, carry):
            pltpu.make_async_remote_copy(
                src_ref=q_buf.at[s, zpeer(d)],
                dst_ref=r_buf.at[s, d - 1],
                send_sem=gz_send.at[s],
                recv_sem=gz_recv.at[s],
                device_id=(gx, zpeer(d)),
                device_id_type=MESH,
            ).start()
            return carry

        each_far(ngz, send)
        r_buf[s, ngz - 1] = q_buf[s, gz]

    def wait_bytes(ref, sem):
        pltpu.make_async_copy(ref, ref, sem).wait()

    def start_gx(s):
        wait_bytes(r_buf.at[s, 0 : ngz - 1], gz_recv.at[s])
        for c in range(3):
            value = r_buf[s, :, c].reshape(t2.shape[1], ny)
            part = jnp.dot(t2[...], value, precision=HIGH, preferred_element_type=jnp.float32)
            for q in range(2):
                p_buf[s, :, c, q, :] = part[q * ngx : (q + 1) * ngx]

        def send(d, carry):
            pltpu.make_async_remote_copy(
                src_ref=p_buf.at[s, xpeer(d)],
                dst_ref=s_buf.at[s, d - 1],
                send_sem=gx_send.at[s],
                recv_sem=gx_recv.at[s],
                device_id=(xpeer(d), gz),
                device_id_type=MESH,
            ).start()
            return carry

        each_far(ngx, send)
        s_buf[s, ngx - 1] = p_buf[s, gx]

    def finish_gx(s):
        wait_bytes(s_buf.at[s, 0 : ngx - 1], gx_recv.at[s])
        coefs = jnp.sum(s_buf[s], axis=0)
        energy = jnp.sum(jnp.sum(coefs * coefs, axis=0), axis=(0, 1), keepdims=True) * (1.0 / ny)
        own = KZ // ngz
        wave = (gx // own) * KZ + gz * own + lax.rem(gx, own)
        energy = jnp.broadcast_to(energy, (1, ny))
        goal = jnp.full((1, ny), target[wave], jnp.float32)
        ratio = (energy - goal) / (energy + goal)
        term[...] += jnp.where(lane[0:1] == s, ratio * ratio, 0.0)

    def local_reward(s):
        offset = interior(s + 1, 0) - mean[...].reshape(1, 1, ny)
        square = offset * offset
        wide = jnp.concatenate([square[x] for x in range(nx)], axis=1)
        pick = (
            lax.broadcasted_iota(jnp.int32, (nx, nx * ny), 1) // ny
            == lax.broadcasted_iota(jnp.int32, (nx, nx * ny), 0)
        ).astype(jnp.float32)
        total = lax.dot_general(
            pick,
            wide,
            (((1,), (1,)), ((), ())),
            precision=HIGH,
            preferred_element_type=jnp.float32,
        )
        loc[s] = total * (-1.0 / ny)

    term[...] = jnp.zeros_like(term)
    load_vel.wait()
    pl.semaphore_wait(barrier, ngx + ngz + 2)
    start_edges(0, 4, field.at[0])
    start_lines(0, 4)
    for load in (load_t1, load_t2, load_mean, load_past, load_boot):
        load.wait()

    def viscosity(s, head, end):
        def each(i, carry):
            part = field[0, 3, i, head:end, :]
            nu[s, i, head:end, :] = BASE_VISCOSITY + part[:, s : s + 1] * wall
            return carry

        lax.fori_loop(0, nx + 2 * HALO + 1, each, 0)

    wait_x(0, 4)
    viscosity(0, 0, nz)

    def body(s, carry):
        stages(s, True)

        @pl.when(s == 0)
        def _():
            wait_z(0, 4)
            viscosity(0, nz, span)

        @pl.when(s >= 1)
        def _():
            wait_z(s, 3)

        stages(s, False)

        @pl.when(s < steps - 1)
        def _():
            start_edges(s + 1, 3, fresh)
            start_lines(s + 1, 3)

        start_gz(s)
        settle(s)
        local_reward(s)
        for later in range(1, steps):
            pl.when(s == later - 1)(functools.partial(viscosity, later, 0, span))

        @pl.when(s >= 1)
        def _():
            start_gx(s - 1)

        @pl.when(s >= 2)
        def _():
            finish_gx(s - 2)

        @pl.when(s < steps - 1)
        def _():
            wait_x(s + 1, 3)

        return carry

    lax.fori_loop(0, steps, body, 0)

    store_vel = pltpu.make_async_copy(
        field.at[steps, 0:3, pl.ds(HALO + 1, nx), 0:nz, :], out_vel, local_sem.at[0]
    )
    store_vel.start()
    start_gx(steps - 1)
    finish_gx(steps - 2)

    plain = [None] * (past_steps + steps)
    running = boot[...]
    for t in range(past_steps + steps - 1, -1, -1):
        reward = past[t] if t < past_steps else loc[t - past_steps]
        running = reward + DISCOUNT * running
        plain[t] = running

    finish_gx(steps - 1)

    def send_x(d, carry):
        pltpu.make_async_remote_copy(
            src_ref=term,
            dst_ref=a_buf.at[d - 1],
            send_sem=ar_send.at[0],
            recv_sem=ar_recv.at[0],
            device_id=(xpeer(d), gz),
            device_id_type=MESH,
        ).start()
        return carry

    each_far(ngx, send_x)
    wait_bytes(a_buf, ar_recv.at[0])
    b_tile[...] = term[...] + jnp.sum(a_buf[...], axis=0)

    def send_z(d, carry):
        pltpu.make_async_remote_copy(
            src_ref=b_tile,
            dst_ref=b_buf.at[d - 1],
            send_sem=ar_send.at[1],
            recv_sem=ar_recv.at[1],
            device_id=(gx, zpeer(d)),
            device_id_type=MESH,
        ).start()
        return carry

    each_far(ngz, send_z)
    wait_bytes(b_buf, ar_recv.at[1])
    spectrum = (b_tile[...] + jnp.sum(b_buf[...], axis=0)) * (-1.0 / KX)

    extra = None
    for t in range(past_steps + steps - 1, -1, -1):
        if extra is not None:
            extra = extra * DISCOUNT
        if t >= past_steps:
            new = spectrum[:, t - past_steps : t - past_steps + 1]
            extra = new if extra is None else extra + new
        out_ret[t] = plain[t] + extra
    store_ret = pltpu.make_async_copy(out_ret, out_hbm, local_sem.at[1])
    store_ret.start()

    def drain(s, carry):
        wait_bytes(r_buf.at[s, 0 : ngz - 1], gz_send.at[s])
        wait_bytes(s_buf.at[s, 0 : ngx - 1], gx_send.at[s])
        return carry

    lax.fori_loop(0, steps, drain, 0)
    wait_sent(0, 4)
    for s in range(1, steps):
        wait_sent(s, 3)
    wait_bytes(a_buf, ar_send.at[0])
    wait_bytes(b_buf, ar_send.at[1])
    store_vel.wait()
    store_ret.wait()


def place(vel, ret, out_vel, out_ret):
    out_vel[...] = vel[...]
    out_ret[...] = ret[...]


def on_device(
    ngx, ngz, velocity, eddy_viscosity, target_spectrum, mean_profile, past_rewards, bootstrap_values
):
    nx, nz, ny = velocity.shape[1:]
    steps = eddy_viscosity.shape[0]
    horizon = past_rewards.shape[0] + steps
    t1 = z_table(ngz, nx, nz, nx * ngx, nz * ngz)
    t2 = x_table(ngx, ngz, nx, nx * ngx)
    span = nz + 2 * HALO
    lines = nx + 2 * HALO + 3
    f32 = jnp.float32
    hbm = pl.BlockSpec(memory_space=pltpu.HBM)
    free = pl.BlockSpec(memory_space=pl.ANY)
    smem = pl.BlockSpec(memory_space=pltpu.SMEM)
    dma = pltpu.SemaphoreType.DMA
    found = pl.pallas_call(
        functools.partial(kernel, ngx, ngz),
        out_shape=(
            jax.ShapeDtypeStruct(velocity.shape, f32),
            jax.ShapeDtypeStruct((horizon, nx, nz), f32),
        ),
        in_specs=[hbm, hbm, smem, hbm, hbm, hbm, hbm, hbm],
        out_specs=(free, free),
        scratch_shapes=[
            pltpu.VMEM(eddy_viscosity.shape, f32),
            pltpu.VMEM((1, ny), f32),
            pltpu.VMEM(past_rewards.shape, f32),
            pltpu.VMEM(bootstrap_values.shape, f32),
            pltpu.VMEM((horizon, nx, nz), f32),
            pltpu.VMEM((3, lines, span, ny), f32),
            pltpu.VMEM((steps + 1, 4, lines, span, ny), f32),
            pltpu.VMEM((3, lines * span, ny), f32),
            pltpu.VMEM((3, lines * span, ny), f32),
            pltpu.VMEM((3, lines * span, ny), f32),
            pltpu.VMEM((steps, lines, span, ny), f32),
            pltpu.VMEM((steps, 2, 4, nx, HALO, ny), f32),
            pltpu.VMEM((steps, 2, 4, nx, HALO, ny), f32),
            pltpu.VMEM((steps, 4, 4, 8, ny), f32),
            pltpu.VMEM((steps, 4, 4, 8, ny), f32),
            pltpu.VMEM(t1.shape[1:], f32),
            pltpu.VMEM(t2.shape[1:], f32),
            pltpu.VMEM((steps, ngz, 3, t1.shape[1] // ngz, ny), f32),
            pltpu.VMEM((steps, ngz, 3, t1.shape[1] // ngz, ny), f32),
            pltpu.VMEM((steps, ngx, 3, 2, ny), f32),
            pltpu.VMEM((steps, ngx, 3, 2, ny), f32),
            pltpu.VMEM((steps, nx, nz), f32),
            pltpu.VMEM((1, ny), f32),
            pltpu.VMEM((ngx - 1, 1, ny), f32),
            pltpu.VMEM((1, ny), f32),
            pltpu.VMEM((ngz - 1, 1, ny), f32),
            dma((7,)),
            dma((steps, 8)),
            dma((steps, 8)),
            dma((steps,)),
            dma((steps,)),
            dma((steps,)),
            dma((steps,)),
            dma((2,)),
            dma((2,)),
        ],
        compiler_params=pltpu.CompilerParams(
            collective_id=0, has_side_effects=True, vmem_limit_bytes=62 * 1024 * 1024
        ),
        name="rollout",
    )(
        velocity,
        eddy_viscosity,
        target_spectrum,
        mean_profile.reshape(1, ny),
        past_rewards,
        bootstrap_values,
        jnp.asarray(t1),
        jnp.asarray(t2),
    )

    return pl.pallas_call(
        place,
        out_shape=tuple(jax.ShapeDtypeStruct(part.shape, f32) for part in found),
        in_specs=[pl.BlockSpec(memory_space=pltpu.VMEM)] * 2,
        out_specs=(pl.BlockSpec(memory_space=pltpu.VMEM),) * 2,
        name="place",
    )(*found)


def solution(mesh):
    placed = (
        P(None, "gx", "gz", None),
        P(None, "gx", "gz"),
        P(),
        P(),
        P(None, "gx", "gz"),
        P("gx", "gz"),
    )
    return jax.shard_map(
        functools.partial(on_device, mesh.shape["gx"], mesh.shape["gz"]),
        mesh=mesh,
        in_specs=placed,
        out_specs=(P(None, "gx", "gz", None), P(None, "gx", "gz")),
        check_vma=False,
    )
```
